1024 devices in a mesh: gx: 128 (over z, x), gy: 8 (over y, core).
Axes of the slice: x: 4, y: 4, z: 32, core: 2. Of those that a mesh axis runs over, the one named last changes fastest.
Arguments:
- adjoint_state: float32 [65536, 1536], P(('gx', 'gy')), may hold values from -6 to 6
- geometry: float32 [65536, 1536], P(('gx', 'gy')), may hold values from 0.5 to 2
- inv_mass: float32 [65536, 512], P(('gx', 'gy')), may hold values from 0.5 to 2
- profile_weight: float32 [65536, 512], P(('gx', 'gy')), may hold values from 0.2 to 10, as said below
- bin_index: int32 [65536, 512], P(('gx', 'gy')), may hold values from 0 to 127
- local_pairs: int32 [40960, 2], P(('gx', 'gy')), may hold values from 0 to 383, as said below
- remote_faces: int32 [10240, 24], P(('gx', 'gy')), may hold values from 0 to 383, as said below
Outputs:
- final_state: float32 [65536, 1536], P(('gx', 'gy'))
- profile_gradient: float32 [3, 128], replicated
The draws below stay inside these ranges and needn't reach their ends.
Inputs may be any that keep to these rules, and one draw needn't show every extreme that they name: `local_pairs`: ids are local face ids 6 e + f of the device's own elements. A device's 40 pairs and its 10 x 24 slots name distinct faces. `remote_faces`: row r of a device's block lists faces shared with its partner at level r; slot k meets the partner's slot k of the same row. Ids are local face ids, distinct from each other and from the device's pair faces. `profile_weight`: weights are positive.
All inputs are finite; a program needn't handle non-finite values.
Results may differ from the reference program's by a relative error of at most 0.0003.
Values sent between devices are 32-bit elements; how exact they have to be, the bound alone decides.
No kernel may reach another device: no remote copies, remote signals or barrier semaphores. Data moves between devices by JAX's collectives and lax.ppermute only.
A program may use at most 32 MiB of HBM per device.

```python
import math
import jax
import jax.numpy as jnp
import numpy as np
from jax import lax

NBIN = 128
E_DEV = 64
K_SLOT = 24
STEPS = 2
GX_BITS = 7
BITS = 10
PAIRS = 40
EL = 65536
N_GX = 128
N_GY = 8


def face_ordering(key):
    devices = EL // E_DEV
    device_keys = jax.random.split(jax.random.fold_in(key, 17), devices)
    return jax.vmap(lambda single: jax.random.permutation(single, 6 * E_DEV))(device_keys).astype(jnp.int32)


def draw_local_pairs(key, part):
    ordering = face_ordering(key)
    return ordering[:, :2 * PAIRS].reshape(-1, 2)


def draw_remote_faces(key, part):
    ordering = face_ordering(key)
    return ordering[:, 2 * PAIRS:2 * PAIRS + BITS * K_SLOT].reshape(-1, K_SLOT)


def draw_profile_weight(key, part):
    ramp = 1.0 + 2.0 * jnp.arange(EL, dtype=jnp.float32)[:, None] / EL
    spread = jnp.exp(jax.random.uniform(key, (EL, 512), jnp.float32, -1.2, 1.2))
    return ramp * spread


def touch_ends(drawn, stream_key, least, largest):
    index_at = [jax.random.randint(jax.random.fold_in(stream_key, axis), (), 0, length) for axis, length in enumerate(drawn.shape)]
    main_axis = drawn.shape.index(max(drawn.shape))
    neighbour = index_at[:main_axis] + [(index_at[main_axis] + 1) % drawn.shape[main_axis]] + index_at[main_axis + 1:]
    return drawn.at[tuple(index_at)].set(least).at[tuple(neighbour)].set(largest)


def block_scale(key, shape, cuts, least, largest):
    loudness, own = 1.0, jax.random.fold_in(key, 6)
    for position, blocks in cuts:
        draws = jnp.exp(jax.random.uniform(jax.random.fold_in(own, position), (blocks,), jnp.float32, least / len(cuts), largest / len(cuts)))
        loudness = loudness * jnp.repeat(draws, shape[position] // blocks).reshape([-1 if axis == position else 1 for axis in range(len(shape))])
    return loudness


def gaussian(rng, dims, width, most, cuts=(), kind=jnp.bfloat16):
    drawn = jax.random.normal(rng, dims, jnp.float32) * width
    if len(cuts) > 0:
        drawn = block_scale(rng, dims, cuts, -0.22, 0.18) * drawn
    return jnp.clip(drawn, min=-most, max=most).astype(kind)


def setup_inputs(seed: int = 0) -> dict:
    arg_keys = jax.random.split(jax.random.key(seed), 8)
    adjoint_state = gaussian(arg_keys[0], (EL, 3 * 512), 1.0, 6.0, ((0, 1024),), jnp.float32)
    geometry = jnp.clip(jnp.exp(math.log(2.0) - 1.3862944 * jax.random.uniform(arg_keys[1], (EL, 3 * 512), jnp.float32) ** block_scale(arg_keys[1], (EL, 3 * 512), ((0, 1024),), -0.2, 0.2)), 0.5, 2.0)
    inv_mass = jnp.clip(jnp.exp(math.log(2.0) - 1.3862944 * jax.random.uniform(arg_keys[2], (EL, 512), jnp.float32) ** block_scale(arg_keys[2], (EL, 512), ((0, 1024),), -0.2, 0.2)), 0.5, 2.0)
    profile_weight = draw_profile_weight(jax.random.fold_in(arg_keys[7], 71), 0)
    bin_index = touch_ends(jax.random.randint(arg_keys[4], (EL, 512), 0, NBIN), jax.random.fold_in(arg_keys[4], 1), 0, NBIN - 1).astype(jnp.int32)
    local_pairs = draw_local_pairs(jax.random.fold_in(arg_keys[7], 71), 0)
    remote_faces = draw_remote_faces(jax.random.fold_in(arg_keys[7], 71), 0)
    return {"adjoint_state": adjoint_state, "geometry": geometry, "inv_mass": inv_mass, "profile_weight": profile_weight, "bin_index": bin_index, "local_pairs": local_pairs, "remote_faces": remote_faces}


precise = lax.Precision.HIGHEST
step_size = 0.00015

def cheb_matrix():
    points = jnp.arange(8)
    nodes = jnp.cos(math.pi * points.astype(jnp.float32) / 7.0)
    weights = jnp.where((points == 0) | (points == 7), 2.0, 1.0).astype(jnp.float32)
    parity = jnp.where((points[:, None] + points[None, :]) % 2 == 0, 1.0, -1.0).astype(jnp.float32)
    spacing = nodes[:, None] - nodes[None, :]
    diagonal_mask = points[:, None] == points[None, :]
    divisor = jnp.where(diagonal_mask, 1.0, spacing)
    offdiag = jnp.where(diagonal_mask, 0.0, weights[:, None] / weights[None, :] * parity / divisor)
    return offdiag - jnp.diag(lax.optimization_barrier(jnp.sum(offdiag, axis=1)))

def stiffness(current, metric, derivative):
    along_k = jnp.einsum('ecijk,lk->ecijl', current, derivative, precision=precise)
    along_j = jnp.einsum('ecijk,lj->ecilk', current, derivative, precision=precise)
    along_i = jnp.einsum('ecijk,li->ecljk', current, derivative, precision=precise)
    result = jnp.einsum('ecijl,lk->ecijk', metric[:, 2:3] * along_k, derivative, precision=precise)
    result = result + jnp.einsum('ecilk,lj->ecijk', metric[:, 1:2] * along_j, derivative, precision=precise)
    result = result + jnp.einsum('ecljk,li->ecijk', metric[:, 0:1] * along_i, derivative, precision=precise)
    return result

def faces_of(stiff):
    count = stiff.shape[0]
    panels = jnp.stack([stiff[:, :, 0], stiff[:, :, 7], stiff[:, :, :, 0], stiff[:, :, :, 7], stiff[:, :, :, :, 0], stiff[:, :, :, :, 7]], axis=1)
    return panels.reshape(count * 6, 192)

def lift_faces(stiff, assembly):
    count = stiff.shape[0]
    pieces = assembly.reshape(count, 6, 3, 8, 8)
    stiff = stiff.at[:, :, 0].add(pieces[:, 0])
    stiff = stiff.at[:, :, 7].add(pieces[:, 1])
    stiff = stiff.at[:, :, :, 0].add(pieces[:, 2])
    stiff = stiff.at[:, :, :, 7].add(pieces[:, 3])
    stiff = stiff.at[:, :, :, :, 0].add(pieces[:, 4])
    stiff = stiff.at[:, :, :, :, 7].add(pieces[:, 5])
    return stiff

def binned(current, profile_weight, bin_index):
    weighted = profile_weight[:, None, :] * current.reshape(EL, 3, 512)
    columns = weighted.transpose(1, 0, 2).reshape(3, EL * 512)
    summed = jax.ops.segment_sum(columns.T, bin_index.reshape(-1), num_segments=NBIN)
    return summed.T

def reference(adjoint_state, geometry, inv_mass, profile_weight, bin_index, local_pairs, remote_faces):
    derivative = cheb_matrix()
    devices = N_GX * N_GY
    current = adjoint_state.reshape(EL, 3, 8, 8, 8)
    metric = geometry.reshape(devices, E_DEV, 3, 8, 8, 8)
    mass_field = inv_mass.reshape(EL, 8, 8, 8)
    pair_base = jnp.arange(devices * PAIRS, dtype=jnp.int32) // PAIRS * (6 * E_DEV)
    global_pairs = local_pairs + pair_base[:, None]
    remote_base = jnp.arange(devices, dtype=jnp.int32) * (6 * E_DEV)
    global_remote = remote_faces.reshape(devices, BITS, K_SLOT) + remote_base[:, None, None]
    device_ids = np.arange(devices)[:, None]
    row_index = np.arange(BITS)[None, :]
    flipped = np.where(row_index < GX_BITS, N_GY * 2 ** row_index, 2 ** np.maximum(row_index - GX_BITS, 0))
    bit_value = device_ids // flipped % 2
    partner = jnp.asarray((device_ids + flipped * (1 - 2 * bit_value)).astype(np.int32))
    levels = jnp.asarray(np.broadcast_to(row_index, (devices, BITS)).astype(np.int32))
    gradient = jnp.zeros((3, NBIN), jnp.float32)
    for section in range(STEPS):
        stiff = lax.map(lambda element: stiffness(element[0], element[1], derivative), (current.reshape(devices, E_DEV, 3, 8, 8, 8), metric))
        stiff = stiff.reshape(EL, 3, 8, 8, 8)
        panels = faces_of(stiff)
        assembly = jnp.zeros_like(panels)
        assembly = assembly.at[global_pairs[:, 0]].add(panels[global_pairs[:, 1]])
        assembly = assembly.at[global_pairs[:, 1]].add(panels[global_pairs[:, 0]])
        outgoing = panels[global_remote]
        received = outgoing[partner, levels]
        assembly = assembly.at[global_remote.reshape(-1)].add(received.reshape(-1, 192))
        current = current - step_size * mass_field[:, None] * lift_faces(stiff, assembly)
        gradient = gradient + binned(current, profile_weight, bin_index)
    scaling = 1.0 / math.sqrt(EL * 512 / NBIN)
    return (current.reshape(EL, 3 * 512), gradient * scaling)
```

```python
import functools
import math

import jax
import jax.numpy as jnp
import numpy as np
from jax import lax
from jax.experimental import pallas as pl
from jax.experimental.pallas import tpu as pltpu
from jax.sharding import Mesh
from jax.sharding import PartitionSpec as P

NBIN = 128
STEP = 0.00015
E = 64
K = 24
F32 = jnp.float32
BF16 = jnp.bfloat16
VM = pltpu.VMEM


def cheb():
    m = np.arange(8)
    x = np.cos(np.pi * m / 7.0)
    c = np.where((m == 0) | (m == 7), 2.0, 1.0)
    sign = np.where((m[:, None] + m[None, :]) % 2 == 0, 1.0, -1.0)
    same = m[:, None] == m[None, :]
    gap = np.where(same, 1.0, x[:, None] - x[None, :])
    off = np.where(same, 0.0, c[:, None] / c[None, :] * sign / gap)
    return off - np.diag(off.sum(axis=1))


def split_const(a):
    hi = a.astype(np.float32).astype(jnp.bfloat16)
    lo = (a - hi.astype(np.float64)).astype(np.float32).astype(jnp.bfloat16)
    return hi, lo


def constants():
    d = cheb()
    last = np.kron(np.eye(16), d.T)
    middle = np.kron(np.kron(np.eye(2), d.T), np.eye(8))
    fh, fl = split_const(np.concatenate([last, middle], axis=1))
    forward = np.concatenate([fh, fh, fl], axis=0)
    bh, bl = split_const(np.concatenate([last.T, middle.T], axis=0))
    back = np.concatenate([bh, bl], axis=1)
    rows = []
    for mat in (d, d.T):
        for cross in (0, 1):
            for out in range(4):
                for src in range(4):
                    low = mat[2 * out, 2 * src + cross]
                    high = mat[2 * out + 1, 2 * src + 1 - cross]
                    rows.append(np.repeat([low, high], 64))
    coef = np.stack(rows).astype(np.float32)
    p = np.arange(64)
    u, l = p // 8, p % 8
    targets = np.concatenate(
        [p, 448 + p, u * 64 + l, u * 64 + 56 + l, u * 64 + l * 8, u * 64 + l * 8 + 7]
    )
    sel = np.arange(512)[:, None] == targets[None, :]
    sel = sel.astype(np.float32).astype(jnp.bfloat16)
    return forward, back, coef, sel, np.ascontiguousarray(sel.T)


def split(x):
    hi = x.astype(BF16)
    return hi, (x - hi.astype(F32)).astype(BF16)


def dot(a, b):
    return lax.dot_general(a, b, (((1,), (0,)), ((), ())), preferred_element_type=F32)


def thrice(x):
    return jnp.concatenate([x, x, x], axis=0)


def stiffness(x, geo, fwd, back, coef):
    quads = [x[:, 128 * q : 128 * q + 128] for q in range(4)]
    rows = jnp.concatenate(quads, axis=0)
    hi, lo = split(rows)
    grads = dot(jnp.concatenate([hi, lo], axis=1), fwd[0:256, :]) + dot(hi, fwd[256:384, :])
    scaled = []
    for q in range(4):
        metric = jnp.concatenate(
            [
                geo[:, 1024 + 128 * q : 1152 + 128 * q],
                geo[:, 512 + 128 * q : 640 + 128 * q],
            ],
            axis=1,
        )
        scaled.append(grads[192 * q : 192 * q + 192] * thrice(metric))
    hi, lo = split(jnp.concatenate(scaled, axis=0))
    both = dot(hi, back[...])
    lanes = both[:, :128] + both[:, 128:] + dot(lo, back[:, 0:128])
    out = []
    for part in range(6):
        lo_row = 32 * part
        e0 = lo_row % 64
        xs = [q[lo_row : lo_row + 32] for q in quads]
        rolled = [pltpu.roll(v, 64, 1) for v in xs]
        mids = []
        for o in range(4):
            acc = None
            for s in range(4):
                r = 4 * o + s
                term = coef[r : r + 1, :] * xs[s] + coef[16 + r : 17 + r, :] * rolled[s]
                acc = term if acc is None else acc + term
            mids.append(acc * geo[e0 : e0 + 32, 128 * o : 128 * o + 128])
        rolled = [pltpu.roll(v, 64, 1) for v in mids]
        cols = []
        for o in range(4):
            base = 192 * o + lo_row
            acc = lanes[base : base + 32]
            for s in range(4):
                r = 32 + 4 * o + s
                acc = acc + coef[r : r + 1, :] * mids[s] + coef[16 + r : 17 + r, :] * rolled[s]
            cols.append(acc)
        out.append(jnp.concatenate(cols, axis=1))
    return jnp.concatenate(out, axis=0)


def store_panels(stiff, extra, sel, pm):
    hi, lo = split(stiff)
    stack = [hi, lo]
    if extra is not None:
        weight, bins = extra
        stack += [*split(weight), bins.astype(BF16)]
    got = dot(jnp.concatenate(stack, axis=0), sel[...])
    face = got[0:192] + got[192:384]
    if extra is not None:
        wface = got[384:448] + got[448:512]
        bface = got[512:576]
    zero = jnp.zeros((E, 64), F32)
    for f in range(6):
        cut = slice(64 * f, 64 * f + 64)
        c0, c1, c2 = (face[64 * c : 64 * c + 64, cut] for c in range(3))
        third = zero if extra is None else wface[:, cut]
        pm[0][pl.ds(f, E, stride=6), :] = jnp.concatenate([c0, c1], axis=1)
        pm[1][pl.ds(f, E, stride=6), :] = jnp.concatenate([c2, third], axis=1)
        if extra is not None:
            pm[2][pl.ds(f, E, stride=6), :] = jnp.concatenate([bface[:, cut], zero], axis=1)


def send_rows(remote, me, levels, pm, out_near, out_far):
    for r, (kind, where) in enumerate(levels):
        for k in range(K):
            face = remote[r, k]
            for i, block in enumerate(pm):
                row, lanes = block[pl.ds(face, 1), :], slice(128 * i, 128 * i + 128)
                if kind == "near":
                    out_near[me[0] ^ where, k : k + 1, lanes] = row
                else:
                    out_far[where][k : k + 1, lanes] = row


def take_rows(remote, me, levels, near, far, asm):
    for r, (kind, where) in enumerate(levels):
        for k in range(K):
            face = remote[r, k]
            for i, block in enumerate(asm):
                lanes = slice(128 * i, 128 * i + 128)
                if kind == "near":
                    row = near[me[0] ^ where, k : k + 1, lanes]
                else:
                    row = far[where][k : k + 1, lanes]
                block[pl.ds(face, 1), :] = row


def pair_rows(pairs, pm, asm):
    for i in range(pairs.shape[0]):
        a, b = pairs[i, 0], pairs[i, 1]
        for source, block in zip(pm, asm):
            block[pl.ds(b, 1), :] = source[pl.ds(a, 1), :]
            block[pl.ds(a, 1), :] = source[pl.ds(b, 1), :]


def lift(asm, selt):
    faces = []
    for f in range(6):
        one = asm[0][pl.ds(f, E, stride=6), :]
        two = asm[1][pl.ds(f, E, stride=6), :]
        faces.append(jnp.concatenate([one[:, 0:64], one[:, 64:128], two[:, 0:64]], axis=0))
    hi, lo = split(jnp.concatenate(faces, axis=1))
    got = dot(jnp.concatenate([hi, lo], axis=0), selt[...])
    return got[0:192] + got[192:384]


def bin_dot(ws, bins):
    groups = bins.shape[0] // 8
    left, right = [], []
    for g in range(groups):
        cut = slice(8 * g, 8 * g + 8)
        b = bins[cut]
        upper, lower = b >> 5, b & 31
        masks = [upper == u for u in range(4)]
        rows = [jnp.where(m, w[cut], 0.0) for w in ws for m in masks]
        left.append(jnp.concatenate(rows, axis=0))
        ones = [jnp.where(lower == v, 1.0, 0.0) for v in range(32)]
        right.append(jnp.concatenate(ones, axis=0).astype(BF16))
    hi, lo = split(jnp.concatenate(left, axis=1))
    return lax.dot_general(
        jnp.concatenate([hi, lo], axis=0),
        jnp.concatenate(right, axis=1),
        (((1,), (1,)), ((), ())),
        preferred_element_type=F32,
    )


def bin_finish(acc):
    row = lax.broadcasted_iota(jnp.int32, (192, 256), 0)
    col = lax.broadcasted_iota(jnp.int32, (192, 256), 1)
    acc = jnp.where((row & 7) == (col & 7), acc, 0.0)
    summed = jnp.sum(acc.reshape(24, 8, 256), axis=1)
    r = lax.broadcasted_iota(jnp.int32, (256, 128), 0)
    c = lax.broadcasted_iota(jnp.int32, (256, 128), 1)
    put = jnp.where((r >> 3) + 64 == c, 1.0, 0.0)
    summed = summed[0:12] + summed[12:24]
    return jnp.dot(summed, put, precision=lax.Precision.HIGHEST, preferred_element_type=F32)


def first_kernel(levels, me, remote, pairs, state, geo, mass, weight, bins, fwd, back, coef, sel, *outs):
    stiff_out, asm0, asm1, out_near, *rest = outs
    out_far, pm = rest[:-3], rest[-3:]
    x = jnp.concatenate([state[:, 512 * c : 512 * c + 512] for c in range(3)], axis=0)
    stiff = stiffness(x, geo, fwd, back, coef)
    stiff_out[...] = stiff
    shares = (-STEP) * weight[...] * mass[...]
    store_panels(stiff, (shares, bins[...].astype(F32)), sel, pm)
    send_rows(remote, me, levels, pm, out_near, out_far)
    asm0[...] = jnp.zeros_like(asm0)
    asm1[...] = jnp.zeros_like(asm1)
    pair_rows(pairs, pm, (asm0, asm1))


def middle_kernel(levels, n_far, me, remote, pairs, *refs):
    near, far = refs[0], refs[1 : 1 + n_far]
    rest = refs[1 + n_far :]
    state, stiff1, asm0, asm1, geo, mass, weight, bins, fwd, back, coef, sel, selt = rest[:13]
    part_out, out_near = rest[13], rest[14]
    out_far = rest[15 : 15 + n_far]
    asm, pm = rest[15 + n_far : 17 + n_far], rest[17 + n_far :]
    asm[0][...] = asm0[...]
    asm[1][...] = asm1[...]
    take_rows(remote, me, levels, near, far, asm)
    scale = thrice(STEP * mass[...])
    x = jnp.concatenate([state[:, 512 * c : 512 * c + 512] for c in range(3)], axis=0)
    x = x - scale * (stiff1[...] + lift(asm, selt))
    stiff = stiffness(x, geo, fwd, back, coef)
    store_panels(stiff, None, sel, pm)
    send_rows(remote, me, levels, pm, out_near, out_far)
    asm[0][...] = jnp.zeros_like(asm0)
    asm[1][...] = jnp.zeros_like(asm1)
    pair_rows(pairs, pm, asm)
    part = x - scale * (stiff + lift(asm, selt))
    part_out[...] = part
    total = x + part
    w = weight[...]
    acc = bin_dot([w * total[64 * c : 64 * c + 64] for c in range(3)], bins[...])
    lane = lax.broadcasted_iota(jnp.int32, (K, 128), 1)
    for r, (kind, where) in enumerate(levels):
        if kind == "near":
            j = me[0] ^ where
            got, sent = (lambda a, b: near[j, :, a:b]), (lambda a, b: out_near[j, :, a:b])
        else:
            got = lambda a, b, ref=far[where]: ref[:, a:b]
            sent = lambda a, b, ref=out_far[where]: ref[:, a:b]
        high, bin_low = got(128, 256), got(256, 384)
        share = jnp.where(lane < 64, pltpu.roll(high, 64, 1), high)
        label = jnp.where(lane < 64, bin_low, pltpu.roll(bin_low, 64, 1)).astype(jnp.int32)
        first = sent(0, 128) * share
        second = jnp.where(lane < 64, sent(128, 256) * share, 0.0)
        fields = [jnp.where(lane < 64, first, 0.0), jnp.where(lane < 64, 0.0, first), second]
        acc = acc + bin_dot(fields, label)
    sums = bin_finish(acc)
    for j in range(out_near.shape[0]):
        out_near[j, 0:12, 192:256] = sums[:, 64:128]


def merge_kernel(copies, near, out):
    sums = jnp.sum(near[:, :, :], axis=0)
    row = lax.broadcasted_iota(jnp.int32, (K, 128), 0)
    col = lax.broadcasted_iota(jnp.int32, (K, 128), 1)
    r = lax.broadcasted_iota(jnp.int32, (128, 128), 0)
    c = lax.broadcasted_iota(jnp.int32, (128, 128), 1)
    spread = jnp.where((r >= 64) & (r < 96) & ((c & 31) == r - 64), 1.0, 0.0)
    sums = jnp.where((row < 12) & (col >= 64) & (col < 96), sums, 0.0)
    full = jnp.dot(sums, spread, precision=lax.Precision.HIGHEST, preferred_element_type=F32)
    full = jnp.where((row & 3) == (col >> 5), full, 0.0)
    done = jnp.concatenate([jnp.sum(full[4 * i : 4 * i + 4], axis=0, keepdims=True) for i in range(3)], axis=0)
    for j in range(copies):
        out[j] = done


def last_kernel(levels, n_far, me, remote, *refs):
    near, far = refs[0], refs[1 : 1 + n_far]
    part, mass, selt, out, *asm = refs[1 + n_far :]
    for block in asm:
        block[...] = jnp.zeros_like(block)
    take_rows(remote, me, levels, near, far, asm)
    moved = part[...] - thrice(STEP * mass[...]) * lift(asm, selt)
    for c in range(3):
        out[:, 512 * c : 512 * c + 512] = moved[64 * c : 64 * c + 64]


SMEM = pl.BlockSpec(memory_space=pltpu.SMEM)
VMEM = pl.BlockSpec(memory_space=pltpu.VMEM)
PARAMS = pltpu.CompilerParams(vmem_limit_bytes=24 * 1024 * 1024)


def on_device(sizes, state, geo, mass, weight, bins, pairs, remote):
    nz, nx, ny, nc = sizes
    group = ("x", "y", "c")
    n_near = nx * ny * nc
    log = lambda n: n.bit_length() - 1
    levels = [("near", ny * nc * 2**b) for b in range(log(nx))]
    levels += [("far", b) for b in range(log(nz))]
    levels += [("near", 2**b) for b in range(log(ny * nc))]
    n_far = log(nz)
    fwd, back, coef, sel, selt = (jnp.asarray(a) for a in constants())
    me = lax.axis_index(group).astype(jnp.int32).reshape(1)
    shape = jax.ShapeDtypeStruct

    def exchange(near, far):
        got_far = [None] * n_far
        for b in reversed(range(n_far)):
            got_far[b] = lax.ppermute(far[b], "z", [(s, s ^ 2**b) for s in range(nz)])
        return lax.all_to_all(near, group, 0, 0, tiled=True), got_far

    stiff1, asm0, asm1, near, *far = pl.pallas_call(
        functools.partial(first_kernel, levels),
        out_shape=[shape((192, 512), F32), shape((384, 128), F32), shape((384, 128), F32)]
        + [shape((n_near, K, 384), F32)] + [shape((K, 384), F32)] * n_far,
        in_specs=[SMEM] * 3 + [VMEM] * 9,
        out_specs=[VMEM] * (4 + n_far),
        scratch_shapes=[VM((384, 128), F32)] * 3,
        compiler_params=PARAMS,
        name="first",
    )(me, remote, pairs, state, geo, mass, weight, bins, fwd, back, coef, sel)
    near, far = exchange(near, far)
    part, near, *far = pl.pallas_call(
        functools.partial(middle_kernel, levels, n_far),
        out_shape=[shape((192, 512), F32), shape((n_near, K, 256), F32)] + [shape((K, 256), F32)] * n_far,
        in_specs=[SMEM] * 3 + [VMEM] * (14 + n_far),
        out_specs=[VMEM] * (2 + n_far),
        scratch_shapes=[VM((384, 128), F32)] * 4,
        compiler_params=PARAMS,
        name="middle",
    )(me, remote, pairs, near, *far, state, stiff1, asm0, asm1, geo, mass, weight, bins, fwd, back, coef, sel, selt)
    near, far = exchange(near, far)
    sums = pl.pallas_call(
        functools.partial(merge_kernel, nz),
        out_shape=shape((nz, 3, 128), F32),
        grid=(1,),
        in_specs=[pl.BlockSpec((n_near, K, 128), lambda i: (0, 0, 1))],
        out_specs=pl.BlockSpec((nz, 3, 128), lambda i: (0, 0, 0)),
        compiler_params=PARAMS,
        name="merge",
    )(near)
    sums = lax.all_to_all(sums, "z", 0, 0, tiled=True)
    final = pl.pallas_call(
        functools.partial(last_kernel, levels, n_far),
        out_shape=shape((E, 1536), F32),
        in_specs=[SMEM] * 2 + [VMEM] * (4 + n_far),
        out_specs=VMEM,
        scratch_shapes=[VM((384, 128), F32)] * 2,
        compiler_params=PARAMS,
        name="last",
    )(me, remote, near, *far, part, mass, selt)
    points = nz * n_near * E * 512
    return final, jnp.sum(sums, axis=0) * (1.0 / math.sqrt(points / NBIN))


def solution(mesh):
    gx, gy = mesh.shape["gx"], mesh.shape["gy"]
    nx = 4 if gx >= 16 else 2
    sizes = (gx // nx, nx, gy // 2, 2)
    names = ("z", "x", "y", "c")
    inner = Mesh(mesh.devices.reshape(sizes), names)
    rows = P(names, None)
    return jax.shard_map(
        functools.partial(on_device, sizes),
        mesh=inner,
        in_specs=(rows,) * 7,
        out_specs=(rows, P()),
        check_vma=False,
    )
```

```python
import functools
import math

import jax
import jax.numpy as jnp
import numpy as np
from jax import lax
from jax.experimental import pallas as pl
from jax.experimental.pallas import tpu as pltpu
from jax.sharding import Mesh
from jax.sharding import PartitionSpec as P

NBIN = 128
STEP = 0.00015
E = 64
K = 24
F32 = jnp.float32
BF16 = jnp.bfloat16
VM = pltpu.VMEM


def cheb():
    m = np.arange(8)
    x = np.cos(np.pi * m / 7.0)
    c = np.where((m == 0) | (m == 7), 2.0, 1.0)
    sign = np.where((m[:, None] + m[None, :]) % 2 == 0, 1.0, -1.0)
    same = m[:, None] == m[None, :]
    gap = np.where(same, 1.0, x[:, None] - x[None, :])
    off = np.where(same, 0.0, c[:, None] / c[None, :] * sign / gap)
    return off - np.diag(off.sum(axis=1))


def split_const(a):
    hi = a.astype(np.float32).astype(jnp.bfloat16)
    lo = (a - hi.astype(np.float64)).astype(np.float32).astype(jnp.bfloat16)
    return hi, lo


def constants():
    d = cheb()
    last = np.kron(np.eye(16), d.T)
    middle = np.kron(np.kron(np.eye(2), d.T), np.eye(8))
    fh, fl = split_const(np.concatenate([last, middle], axis=1))
    forward = np.concatenate([fh, fh, fl], axis=0)
    bh, bl = split_const(np.concatenate([last.T, middle.T], axis=0))
    back = np.concatenate([bh, bl], axis=1)
    rows = []
    for mat in (d, d.T):
        for cross in (0, 1):
            for out in range(4):
                for src in range(4):
                    low = mat[2 * out, 2 * src + cross]
                    high = mat[2 * out + 1, 2 * src + 1 - cross]
                    rows.append(np.repeat([low, high], 64))
    coef = np.stack(rows).astype(np.float32)
    p = np.arange(64)
    u, l = p // 8, p % 8
    targets = np.concatenate(
        [p, 448 + p, u * 64 + l, u * 64 + 56 + l, u * 64 + l * 8, u * 64 + l * 8 + 7]
    )
    sel = np.arange(512)[:, None] == targets[None, :]
    sel = sel.astype(np.float32).astype(jnp.bfloat16)
    return forward, back, coef, sel, np.ascontiguousarray(sel.T)


def split(x):
    hi = x.astype(BF16)
    return hi, (x - hi.astype(F32)).astype(BF16)


def dot(a, b):
    return lax.dot_general(a, b, (((1,), (0,)), ((), ())), preferred_element_type=F32)


def thrice(x):
    return jnp.concatenate([x, x, x], axis=0)


def stiffness(x, geo, fwd, back, coef):
    quads = [x[:, 128 * q : 128 * q + 128] for q in range(4)]
    rows = jnp.concatenate(quads, axis=0)
    hi, lo = split(rows)
    grads = dot(jnp.concatenate([hi, lo], axis=1), fwd[0:256, :]) + dot(hi, fwd[256:384, :])
    scaled = []
    for q in range(4):
        metric = jnp.concatenate(
            [
                geo[:, 1024 + 128 * q : 1152 + 128 * q],
                geo[:, 512 + 128 * q : 640 + 128 * q],
            ],
            axis=1,
        )
        scaled.append(grads[192 * q : 192 * q + 192] * thrice(metric))
    hi, lo = split(jnp.concatenate(scaled, axis=0))
    both = dot(hi, back[...])
    lanes = both[:, :128] + both[:, 128:] + dot(lo, back[:, 0:128])
    out = []
    for part in range(6):
        lo_row = 32 * part
        e0 = lo_row % 64
        xs = [q[lo_row : lo_row + 32] for q in quads]
        rolled = [pltpu.roll(v, 64, 1) for v in xs]
        mids = []
        for o in range(4):
            acc = None
            for s in range(4):
                r = 4 * o + s
                term = coef[r : r + 1, :] * xs[s] + coef[16 + r : 17 + r, :] * rolled[s]
                acc = term if acc is None else acc + term
            mids.append(acc * geo[e0 : e0 + 32, 128 * o : 128 * o + 128])
        rolled = [pltpu.roll(v, 64, 1) for v in mids]
        cols = []
        for o in range(4):
            base = 192 * o + lo_row
            acc = lanes[base : base + 32]
            for s in range(4):
                r = 32 + 4 * o + s
                acc = acc + coef[r : r + 1, :] * mids[s] + coef[16 + r : 17 + r, :] * rolled[s]
            cols.append(acc)
        out.append(jnp.concatenate(cols, axis=1))
    return jnp.concatenate(out, axis=0)


def store_panels(stiff, extra, sel, pm):
    hi, lo = split(stiff)
    stack = [hi, lo]
    if extra is not None:
        weight, bins = extra
        stack += [*split(weight), bins.astype(BF16)]
    got = dot(jnp.concatenate(stack, axis=0), sel[...])
    face = got[0:192] + got[192:384]
    if extra is not None:
        wface = got[384:448] + got[448:512]
        bface = got[512:576]
    zero = jnp.zeros((E, 64), F32)
    for f in range(6):
        cut = slice(64 * f, 64 * f + 64)
        c0, c1, c2 = (face[64 * c : 64 * c + 64, cut] for c in range(3))
        third = zero if extra is None else wface[:, cut]
        pm[0][pl.ds(f, E, stride=6), :] = jnp.concatenate([c0, c1], axis=1)
        pm[1][pl.ds(f, E, stride=6), :] = jnp.concatenate([c2, third], axis=1)
        if extra is not None:
            pm[2][pl.ds(f, E, stride=6), :] = jnp.concatenate([bface[:, cut], zero], axis=1)


def send_rows(remote, me, levels, pm, out_near, out_far):
    for r, (kind, where) in enumerate(levels):
        for k in range(K):
            face = remote[r, k]
            for i, block in enumerate(pm):
                row, lanes = block[pl.ds(face, 1), :], slice(128 * i, 128 * i + 128)
                if kind == "near":
                    out_near[me[0] ^ where, k : k + 1, lanes] = row
                else:
                    out_far[where][k : k + 1, lanes] = row


def take_rows(remote, me, levels, near, far, asm):
    for r, (kind, where) in enumerate(levels):
        for k in range(K):
            face = remote[r, k]
            for i, block in enumerate(asm):
                lanes = slice(128 * i, 128 * i + 128)
                if kind == "near":
                    row = near[me[0] ^ where, k : k + 1, lanes]
                else:
                    row = far[where][k : k + 1, lanes]
                block[pl.ds(face, 1), :] = row


def pair_rows(pairs, pm, asm):
    for i in range(pairs.shape[1]):
        a, b = pairs[0, i], pairs[1, i]
        for source, block in zip(pm, asm):
            block[pl.ds(b, 1), :] = source[pl.ds(a, 1), :]
            block[pl.ds(a, 1), :] = source[pl.ds(b, 1), :]


def lift(asm, selt):
    faces = []
    for f in range(6):
        one = asm[0][pl.ds(f, E, stride=6), :]
        two = asm[1][pl.ds(f, E, stride=6), :]
        faces.append(jnp.concatenate([one[:, 0:64], one[:, 64:128], two[:, 0:64]], axis=0))
    hi, lo = split(jnp.concatenate(faces, axis=1))
    got = dot(jnp.concatenate([hi, lo], axis=0), selt[...])
    return got[0:192] + got[192:384]


def bin_dot(ws, bins):
    groups = bins.shape[0] // 8
    left, right = [], []
    for g in range(groups):
        cut = slice(8 * g, 8 * g + 8)
        b = bins[cut]
        upper, lower = b >> 5, b & 31
        masks = [upper == u for u in range(4)]
        rows = [jnp.where(m, w[cut], 0.0) for w in ws for m in masks]
        left.append(jnp.concatenate(rows, axis=0))
        ones = [jnp.where(lower == v, 1.0, 0.0) for v in range(32)]
        right.append(jnp.concatenate(ones, axis=0).astype(BF16))
    hi, lo = split(jnp.concatenate(left, axis=1))
    return lax.dot_general(
        jnp.concatenate([hi, lo], axis=0),
        jnp.concatenate(right, axis=1),
        (((1,), (1,)), ((), ())),
        preferred_element_type=F32,
    )


def bin_finish(acc):
    row = lax.broadcasted_iota(jnp.int32, (192, 256), 0)
    col = lax.broadcasted_iota(jnp.int32, (192, 256), 1)
    acc = jnp.where((row & 7) == (col & 7), acc, 0.0)
    summed = jnp.sum(acc.reshape(24, 8, 256), axis=1)
    r = lax.broadcasted_iota(jnp.int32, (256, 128), 0)
    c = lax.broadcasted_iota(jnp.int32, (256, 128), 1)
    put = jnp.where((r >> 3) + 64 == c, 1.0, 0.0)
    summed = summed[0:12] + summed[12:24]
    return jnp.dot(summed, put, precision=lax.Precision.HIGHEST, preferred_element_type=F32)


def first_kernel(levels, me, remote, pairs, state, geo, mass, weight, bins, fwd, back, coef, sel, *outs):
    stiff_out, asm0, asm1, out_near, *rest = outs
    out_far, pm = rest[:-3], rest[-3:]
    x = jnp.concatenate([state[:, 512 * c : 512 * c + 512] for c in range(3)], axis=0)
    stiff = stiffness(x, geo, fwd, back, coef)
    stiff_out[...] = stiff
    shares = (-STEP) * weight[...] * mass[...]
    store_panels(stiff, (shares, bins[...].astype(F32)), sel, pm)
    send_rows(remote, me, levels, pm, out_near, out_far)
    asm0[...] = jnp.zeros_like(asm0)
    asm1[...] = jnp.zeros_like(asm1)
    pair_rows(pairs, pm, (asm0, asm1))


def middle_kernel(levels, n_far, me, remote, pairs, *refs):
    near, far = refs[0], refs[1 : 1 + n_far]
    rest = refs[1 + n_far :]
    state, stiff1, asm0, asm1, geo, mass, weight, bins, fwd, back, coef, sel, selt = rest[:13]
    part_out, out_near = rest[13], rest[14]
    out_far = rest[15 : 15 + n_far]
    asm, pm = rest[15 + n_far : 17 + n_far], rest[17 + n_far :]
    asm[0][...] = asm0[...]
    asm[1][...] = asm1[...]
    take_rows(remote, me, levels, near, far, asm)
    scale = thrice(STEP * mass[...])
    x = jnp.concatenate([state[:, 512 * c : 512 * c + 512] for c in range(3)], axis=0)
    x = x - scale * (stiff1[...] + lift(asm, selt))
    stiff = stiffness(x, geo, fwd, back, coef)
    store_panels(stiff, None, sel, pm)
    send_rows(remote, me, levels, pm, out_near, out_far)
    asm[0][...] = jnp.zeros_like(asm0)
    asm[1][...] = jnp.zeros_like(asm1)
    pair_rows(pairs, pm, asm)
    part = x - scale * (stiff + lift(asm, selt))
    part_out[...] = part
    total = x + part
    w = weight[...]
    acc = bin_dot([w * total[64 * c : 64 * c + 64] for c in range(3)], bins[...])
    lane = lax.broadcasted_iota(jnp.int32, (K, 128), 1)
    for r, (kind, where) in enumerate(levels):
        if kind == "near":
            j = me[0] ^ where
            got, sent = (lambda a, b: near[j, :, a:b]), (lambda a, b: out_near[j, :, a:b])
        else:
            got = lambda a, b, ref=far[where]: ref[:, a:b]
            sent = lambda a, b, ref=out_far[where]: ref[:, a:b]
        high, bin_low = got(128, 256), got(256, 384)
        share = jnp.where(lane < 64, pltpu.roll(high, 64, 1), high)
        label = jnp.where(lane < 64, bin_low, pltpu.roll(bin_low, 64, 1)).astype(jnp.int32)
        first = sent(0, 128) * share
        second = jnp.where(lane < 64, sent(128, 256) * share, 0.0)
        fields = [jnp.where(lane < 64, first, 0.0), jnp.where(lane < 64, 0.0, first), second]
        acc = acc + bin_dot(fields, label)
    sums = bin_finish(acc)
    for j in range(out_near.shape[0]):
        out_near[j, 0:12, 192:256] = sums[:, 64:128]


def merge_kernel(copies, n_in, near, *refs):
    out = refs[n_in]
    sums = jnp.sum(near[:, :, :], axis=0)
    row = lax.broadcasted_iota(jnp.int32, (K, 128), 0)
    col = lax.broadcasted_iota(jnp.int32, (K, 128), 1)
    r = lax.broadcasted_iota(jnp.int32, (128, 128), 0)
    c = lax.broadcasted_iota(jnp.int32, (128, 128), 1)
    spread = jnp.where((r >= 64) & (r < 96) & ((c & 31) == r - 64), 1.0, 0.0)
    sums = jnp.where((row < 12) & (col >= 64) & (col < 96), sums, 0.0)
    full = jnp.dot(sums, spread, precision=lax.Precision.HIGHEST, preferred_element_type=F32)
    full = jnp.where((row & 3) == (col >> 5), full, 0.0)
    done = jnp.concatenate([jnp.sum(full[4 * i : 4 * i + 4], axis=0, keepdims=True) for i in range(3)], axis=0)
    for j in range(copies):
        out[j] = done


def last_kernel(levels, n_far, me, remote, *refs):
    near, far = refs[0], refs[1 : 1 + n_far]
    part, mass, selt, out, *asm = refs[1 + n_far :]
    for block in asm:
        block[...] = jnp.zeros_like(block)
    take_rows(remote, me, levels, near, far, asm)
    moved = part[...] - thrice(STEP * mass[...]) * lift(asm, selt)
    for c in range(3):
        out[:, 512 * c : 512 * c + 512] = moved[64 * c : 64 * c + 64]


SMEM = pl.BlockSpec(memory_space=pltpu.SMEM)
ANY = pl.BlockSpec(memory_space=pl.ANY)
PARAMS = pltpu.CompilerParams(vmem_limit_bytes=56 * 1024 * 1024)


def whole(a):
    return pl.BlockSpec(a.shape, lambda i, n=len(a.shape): (0,) * n)


def call(kernel, name, scalars, arrays, outs, scratch):
    return pl.pallas_call(
        kernel,
        out_shape=outs,
        grid=(1,),
        in_specs=[SMEM] * len(scalars) + [whole(a) for a in arrays],
        out_specs=[whole(a) for a in outs],
        scratch_shapes=scratch,
        compiler_params=PARAMS,
        name=name,
    )(*scalars, *arrays)


def on_device(sizes, state, geo, mass, weight, bins, pairs, remote):
    nz, nx, ny, nc = sizes
    group = ("x", "y", "c")
    n_near = nx * ny * nc
    log = lambda n: n.bit_length() - 1
    n_far = log(nz)
    levels = [("near", ny * nc * 2**b) for b in range(log(nx))]
    levels += [("far", n_far - 1 - b) for b in range(n_far)]
    levels += [("near", 2**b) for b in range(log(ny * nc))]
    fwd, back, coef, sel, selt = (jnp.asarray(a) for a in constants())
    me = lax.axis_index(group).astype(jnp.int32).reshape(1)
    shape = lambda *dims: jax.ShapeDtypeStruct(dims, F32)

    def swap(far, first=0):
        masks = [2 ** (n_far - 1 - first - i) for i in range(len(far))]
        return [lax.ppermute(v, "z", [(s, s ^ m) for s in range(nz)]) for v, m in zip(far, masks)]

    def spread(near):
        return lax.all_to_all(near, group, 0, 0, tiled=True)

    ops = [fwd, back, coef, sel]
    stiff1, asm0, asm1, near, *far = call(
        functools.partial(first_kernel, levels),
        "first",
        [me, remote, pairs.T],
        [state, geo, mass, weight, bins, *ops],
        [shape(192, 512), shape(384, 128), shape(384, 128), shape(n_near, K, 384)]
        + [shape(K, 384)] * n_far,
        [VM((384, 128), F32)] * 3,
    )
    near, far = spread(near), swap(far)
    part, near, *far = call(
        functools.partial(middle_kernel, levels, n_far),
        "middle",
        [me, remote, pairs.T],
        [near, *far, state, stiff1, asm0, asm1, geo, mass, weight, bins, *ops, selt],
        [shape(192, 512), shape(n_near, K, 256)] + [shape(K, 256)] * n_far,
        [VM((384, 128), F32)] * 4,
    )
    near, early, late = spread(near), swap(far[:2]), far[2:]
    sums, *late = pl.pallas_call(
        functools.partial(merge_kernel, nz, len(early) + len(late)),
        out_shape=[shape(nz, 3, 128)] + [shape(K, 256)] * len(late),
        grid=(1,),
        in_specs=[pl.BlockSpec((n_near, K, 128), lambda i: (0, 0, 1))] + [ANY] * (len(early) + len(late)),
        out_specs=[pl.BlockSpec((nz, 3, 128), lambda i: (0, 0, 0))] + [ANY] * len(late),
        input_output_aliases={1 + len(early) + i: 1 + i for i in range(len(late))},
        compiler_params=PARAMS,
        name="merge",
    )(near, *early, *late)
    sums = lax.all_to_all(sums, "z", 0, 0, tiled=True)
    far = early + swap(late, 2)
    (final,) = call(
        functools.partial(last_kernel, levels, n_far),
        "last",
        [me, remote],
        [near, *far, part, mass, selt],
        [shape(E, 1536)],
        [VM((384, 128), F32)] * 2,
    )
    points = nz * n_near * E * 512
    return final, jnp.sum(sums, axis=0) * (1.0 / math.sqrt(points / NBIN))


def solution(mesh):
    gx, gy = mesh.shape["gx"], mesh.shape["gy"]
    nx = 4 if gx >= 16 else 2
    sizes = (gx // nx, nx, gy // 2, 2)
    names = ("z", "x", "y", "c")
    inner = Mesh(mesh.devices.reshape(sizes), names)
    rows = P(names, None)
    return jax.shard_map(
        functools.partial(on_device, sizes),
        mesh=inner,
        in_specs=(rows,) * 7,
        out_specs=(rows, P()),
        check_vma=False,
    )
```

```python
import functools
import math

import jax
import jax.numpy as jnp
import numpy as np
from jax import lax
from jax.experimental import pallas as pl
from jax.experimental.pallas import tpu as pltpu
from jax.sharding import Mesh
from jax.sharding import PartitionSpec as P

NBIN = 128
STEP = 0.00015
E = 64
K = 24
F32 = jnp.float32
BF16 = jnp.bfloat16
VM = pltpu.VMEM


def cheb():
    m = np.arange(8)
    x = np.cos(np.pi * m / 7.0)
    c = np.where((m == 0) | (m == 7), 2.0, 1.0)
    sign = np.where((m[:, None] + m[None, :]) % 2 == 0, 1.0, -1.0)
    same = m[:, None] == m[None, :]
    gap = np.where(same, 1.0, x[:, None] - x[None, :])
    off = np.where(same, 0.0, c[:, None] / c[None, :] * sign / gap)
    return off - np.diag(off.sum(axis=1))


def split_const(a):
    hi = a.astype(np.float32).astype(jnp.bfloat16)
    lo = (a - hi.astype(np.float64)).astype(np.float32).astype(jnp.bfloat16)
    return hi, lo


def constants():
    d = cheb()
    last = np.kron(np.eye(16), d.T)
    middle = np.kron(np.kron(np.eye(2), d.T), np.eye(8))
    fh, fl = split_const(np.concatenate([last, middle], axis=1))
    forward = np.concatenate([fh, fh, fl], axis=0)
    bh, bl = split_const(np.concatenate([last.T, middle.T], axis=0))
    back = np.concatenate([bh, bl], axis=1)
    rows = []
    for mat in (d, d.T):
        for cross in (0, 1):
            for out in range(4):
                for src in range(4):
                    low = mat[2 * out, 2 * src + cross]
                    high = mat[2 * out + 1, 2 * src + 1 - cross]
                    rows.append(np.repeat([low, high], 64))
    coef = np.stack(rows).astype(np.float32)
    p = np.arange(64)
    u, l = p // 8, p % 8
    targets = np.concatenate(
        [p, 448 + p, u * 64 + l, u * 64 + 56 + l, u * 64 + l * 8, u * 64 + l * 8 + 7]
    )
    sel = np.arange(512)[:, None] == targets[None, :]
    sel = sel.astype(np.float32).astype(jnp.bfloat16)
    return forward, back, coef, sel, np.ascontiguousarray(sel.T)


def split(x):
    hi = x.astype(BF16)
    return hi, (x - hi.astype(F32)).astype(BF16)


def dot(a, b):
    return lax.dot_general(a, b, (((1,), (0,)), ((), ())), preferred_element_type=F32)


def thrice(x):
    return jnp.concatenate([x, x, x], axis=0)


def stiffness(x, geo, fwd, back, coef):
    quads = [x[:, 128 * q : 128 * q + 128] for q in range(4)]
    rows = jnp.concatenate(quads, axis=0)
    hi, lo = split(rows)
    grads = dot(jnp.concatenate([hi, lo], axis=1), fwd[0:256, :]) + dot(hi, fwd[256:384, :])
    scaled = []
    for q in range(4):
        metric = jnp.concatenate(
            [
                geo[:, 1024 + 128 * q : 1152 + 128 * q],
                geo[:, 512 + 128 * q : 640 + 128 * q],
            ],
            axis=1,
        )
        scaled.append(grads[192 * q : 192 * q + 192] * thrice(metric))
    hi, lo = split(jnp.concatenate(scaled, axis=0))
    both = dot(hi, back[...])
    lanes = both[:, :128] + both[:, 128:] + dot(lo, back[:, 0:128])
    out = []
    for part in range(6):
        lo_row = 32 * part
        e0 = lo_row % 64
        xs = [q[lo_row : lo_row + 32] for q in quads]
        rolled = [pltpu.roll(v, 64, 1) for v in xs]
        mids = []
        for o in range(4):
            acc = None
            for s in range(4):
                r = 4 * o + s
                term = coef[r : r + 1, :] * xs[s] + coef[16 + r : 17 + r, :] * rolled[s]
                acc = term if acc is None else acc + term
            mids.append(acc * geo[e0 : e0 + 32, 128 * o : 128 * o + 128])
        rolled = [pltpu.roll(v, 64, 1) for v in mids]
        cols = []
        for o in range(4):
            base = 192 * o + lo_row
            acc = lanes[base : base + 32]
            for s in range(4):
                r = 32 + 4 * o + s
                acc = acc + coef[r : r + 1, :] * mids[s] + coef[16 + r : 17 + r, :] * rolled[s]
            cols.append(acc)
        out.append(jnp.concatenate(cols, axis=1))
    return jnp.concatenate(out, axis=0)


def store_panels(stiff, extra, sel, pm):
    hi, lo = split(stiff)
    stack = [hi, lo]
    if extra is not None:
        weight, bins = extra
        stack += [*split(weight), bins.astype(BF16)]
    got = dot(jnp.concatenate(stack, axis=0), sel[...])
    face = got[0:192] + got[192:384]
    if extra is not None:
        wface = got[384:448] + got[448:512]
        bface = got[512:576]
    zero = jnp.zeros((E, 64), F32)
    for f in range(6):
        cut = slice(64 * f, 64 * f + 64)
        c0, c1, c2 = (face[64 * c : 64 * c + 64, cut] for c in range(3))
        third = zero if extra is None else wface[:, cut]
        pm[0][pl.ds(f, E, stride=6), :] = jnp.concatenate([c0, c1], axis=1)
        pm[1][pl.ds(f, E, stride=6), :] = jnp.concatenate([c2, third], axis=1)
        if extra is not None:
            pm[2][pl.ds(f, E, stride=6), :] = jnp.concatenate([bface[:, cut], zero], axis=1)


def send_rows(remote, me, levels, pm, out_near, out_far):
    for r, (kind, where) in enumerate(levels):
        for k in range(K):
            face = remote[r, k]
            for i, block in enumerate(pm):
                row, lanes = block[pl.ds(face, 1), :], slice(128 * i, 128 * i + 128)
                if kind == "near":
                    out_near[me[0] ^ where, k : k + 1, lanes] = row
                else:
                    out_far[where][k : k + 1, lanes] = row


def take_rows(remote, me, levels, near, far, asm):
    for r, (kind, where) in enumerate(levels):
        for k in range(K):
            face = remote[r, k]
            for i, block in enumerate(asm):
                lanes = slice(128 * i, 128 * i + 128)
                if kind == "near":
                    row = near[me[0] ^ where, k : k + 1, lanes]
                else:
                    row = far[where][k : k + 1, lanes]
                block[pl.ds(face, 1), :] = row


def pair_rows(pairs, pm, asm):
    for i in range(pairs.shape[1]):
        a, b = pairs[0, i], pairs[1, i]
        for source, block in zip(pm, asm):
            block[pl.ds(b, 1), :] = source[pl.ds(a, 1), :]
            block[pl.ds(a, 1), :] = source[pl.ds(b, 1), :]


def lift(asm, selt):
    faces = []
    for f in range(6):
        one = asm[0][pl.ds(f, E, stride=6), :]
        two = asm[1][pl.ds(f, E, stride=6), :]
        faces.append(jnp.concatenate([one[:, 0:64], one[:, 64:128], two[:, 0:64]], axis=0))
    hi, lo = split(jnp.concatenate(faces, axis=1))
    got = dot(jnp.concatenate([hi, lo], axis=0), selt[...])
    return got[0:192] + got[192:384]


def bin_dot(ws, bins):
    groups = bins.shape[0] // 8
    left, right = [], []
    for g in range(groups):
        cut = slice(8 * g, 8 * g + 8)
        b = bins[cut]
        upper, lower = b >> 5, b & 31
        masks = [upper == u for u in range(4)]
        rows = [jnp.where(m, w[cut], 0.0) for w in ws for m in masks]
        left.append(jnp.concatenate(rows, axis=0))
        ones = [jnp.where(lower == v, 1.0, 0.0) for v in range(32)]
        right.append(jnp.concatenate(ones, axis=0).astype(BF16))
    hi, lo = split(jnp.concatenate(left, axis=1))
    return lax.dot_general(
        jnp.concatenate([hi, lo], axis=0),
        jnp.concatenate(right, axis=1),
        (((1,), (1,)), ((), ())),
        preferred_element_type=F32,
    )


def bin_finish(acc):
    row = lax.broadcasted_iota(jnp.int32, (192, 256), 0)
    col = lax.broadcasted_iota(jnp.int32, (192, 256), 1)
    acc = jnp.where((row & 7) == (col & 7), acc, 0.0)
    summed = jnp.sum(acc.reshape(24, 8, 256), axis=1)
    r = lax.broadcasted_iota(jnp.int32, (256, 128), 0)
    c = lax.broadcasted_iota(jnp.int32, (256, 128), 1)
    put = jnp.where((r >> 3) + 64 == c, 1.0, 0.0)
    summed = summed[0:12] + summed[12:24]
    return jnp.dot(summed, put, precision=lax.Precision.HIGHEST, preferred_element_type=F32)


def first_kernel(levels, me, remote, pairs, state, geo, mass, weight, bins, fwd, back, coef, sel, *outs):
    stiff_out, asm0, asm1, out_near, *rest = outs
    out_far, pm = rest[:-3], rest[-3:]
    x = jnp.concatenate([state[:, 512 * c : 512 * c + 512] for c in range(3)], axis=0)
    stiff = stiffness(x, geo, fwd, back, coef)
    stiff_out[...] = stiff
    shares = (-STEP) * weight[...] * mass[...]
    store_panels(stiff, (shares, bins[...].astype(F32)), sel, pm)
    send_rows(remote, me, levels, pm, out_near, out_far)
    asm0[...] = jnp.zeros_like(asm0)
    asm1[...] = jnp.zeros_like(asm1)
    pair_rows(pairs, pm, (asm0, asm1))


def middle_kernel(levels, n_far, me, remote, pairs, *refs):
    near, far = refs[0], refs[1 : 1 + n_far]
    rest = refs[1 + n_far :]
    state, stiff1, asm0, asm1, geo, mass, weight, bins, fwd, back, coef, sel, selt = rest[:13]
    part_out, out_near = rest[13], rest[14]
    out_far = rest[15 : 15 + n_far]
    asm, pm = rest[15 + n_far : 17 + n_far], rest[17 + n_far :]
    asm[0][...] = asm0[...]
    asm[1][...] = asm1[...]
    take_rows(remote, me, levels, near, far, asm)
    scale = thrice(STEP * mass[...])
    x = jnp.concatenate([state[:, 512 * c : 512 * c + 512] for c in range(3)], axis=0)
    x = x - scale * (stiff1[...] + lift(asm, selt))
    stiff = stiffness(x, geo, fwd, back, coef)
    store_panels(stiff, None, sel, pm)
    send_rows(remote, me, levels, pm, out_near, out_far)
    asm[0][...] = jnp.zeros_like(asm0)
    asm[1][...] = jnp.zeros_like(asm1)
    pair_rows(pairs, pm, asm)
    part = x - scale * (stiff + lift(asm, selt))
    part_out[...] = part
    total = x + part
    w = weight[...]
    acc = bin_dot([w * total[64 * c : 64 * c + 64] for c in range(3)], bins[...])
    lane = lax.broadcasted_iota(jnp.int32, (K, 128), 1)
    for r, (kind, where) in enumerate(levels):
        if kind == "near":
            j = me[0] ^ where
            got, sent = (lambda a, b: near[j, :, a:b]), (lambda a, b: out_near[j, :, a:b])
        else:
            got = lambda a, b, ref=far[where]: ref[:, a:b]
            sent = lambda a, b, ref=out_far[where]: ref[:, a:b]
        high, bin_low = got(128, 256), got(256, 384)
        share = jnp.where(lane < 64, pltpu.roll(high, 64, 1), high)
        label = jnp.where(lane < 64, bin_low, pltpu.roll(bin_low, 64, 1)).astype(jnp.int32)
        first = sent(0, 128) * share
        second = jnp.where(lane < 64, sent(128, 256) * share, 0.0)
        fields = [jnp.where(lane < 64, first, 0.0), jnp.where(lane < 64, 0.0, first), second]
        acc = acc + bin_dot(fields, label)
    sums = bin_finish(acc)
    for j in range(out_near.shape[0]):
        out_near[j, 0:12, 192:256] = sums[:, 64:128]


def merge_kernel(copies, n_in, near, *refs):
    out = refs[n_in]
    sums = jnp.sum(near[:, :, :], axis=0)
    row = lax.broadcasted_iota(jnp.int32, (K, 128), 0)
    col = lax.broadcasted_iota(jnp.int32, (K, 128), 1)
    r = lax.broadcasted_iota(jnp.int32, (128, 128), 0)
    c = lax.broadcasted_iota(jnp.int32, (128, 128), 1)
    spread = jnp.where((r >= 64) & (r < 96) & ((c & 31) == r - 64), 1.0, 0.0)
    sums = jnp.where((row < 12) & (col >= 64) & (col < 96), sums, 0.0)
    full = jnp.dot(sums, spread, precision=lax.Precision.HIGHEST, preferred_element_type=F32)
    full = jnp.where((row & 3) == (col >> 5), full, 0.0)
    done = jnp.concatenate([jnp.sum(full[4 * i : 4 * i + 4], axis=0, keepdims=True) for i in range(3)], axis=0)
    for j in range(copies):
        out[j] = done


def last_kernel(levels, n_far, me, remote, *refs):
    near, far = refs[0], refs[1 : 1 + n_far]
    part, mass, selt, out, *asm = refs[1 + n_far :]
    for block in asm:
        block[...] = jnp.zeros_like(block)
    take_rows(remote, me, levels, near, far, asm)
    moved = part[...] - thrice(STEP * mass[...]) * lift(asm, selt)
    for c in range(3):
        out[:, 512 * c : 512 * c + 512] = moved[64 * c : 64 * c + 64]


SMEM = pl.BlockSpec(memory_space=pltpu.SMEM)
ANY = pl.BlockSpec(memory_space=pl.ANY)
PARAMS = pltpu.CompilerParams(vmem_limit_bytes=56 * 1024 * 1024)


def whole(a):
    return pl.BlockSpec(a.shape, lambda i, n=len(a.shape): (0,) * n)


def call(kernel, name, scalars, arrays, outs, scratch):
    return pl.pallas_call(
        kernel,
        out_shape=outs,
        grid=(1,),
        in_specs=[SMEM] * len(scalars) + [whole(a) for a in arrays],
        out_specs=[whole(a) for a in outs],
        scratch_shapes=scratch,
        compiler_params=PARAMS,
        name=name,
    )(*scalars, *arrays)


def on_device(sizes, state, geo, mass, weight, bins, pairs, remote):
    nz, nx, ny, nc = sizes
    group = ("x", "y", "c")
    n_near = nx * ny * nc
    log = lambda n: n.bit_length() - 1
    n_far = log(nz)
    levels = [("near", ny * nc * 2**b) for b in range(log(nx))]
    levels += [("far", n_far - 1 - b) for b in range(n_far)]
    levels += [("near", 2**b) for b in range(log(ny * nc))]
    fwd, back, coef, sel, selt = (jnp.asarray(a) for a in constants())
    me = lax.axis_index(group).astype(jnp.int32).reshape(1)
    shape = lambda *dims: jax.ShapeDtypeStruct(dims, F32)

    def swap(far, first=0):
        masks = [2 ** (n_far - 1 - first - i) for i in range(len(far))]
        return [lax.ppermute(v, "z", [(s, s ^ m) for s in range(nz)]) for v, m in zip(far, masks)]

    def spread(near):
        return lax.all_to_all(near, group, 0, 0, tiled=True)

    ops = [fwd, back, coef, sel]
    stiff1, asm0, asm1, near, *far = call(
        functools.partial(first_kernel, levels),
        "first",
        [me, remote, pairs.T],
        [state, geo, mass, weight, bins, *ops],
        [shape(192, 512), shape(384, 128), shape(384, 128), shape(n_near, K, 384)]
        + [shape(K, 384)] * n_far,
        [VM((384, 128), F32)] * 3,
    )
    near, far = spread(near), swap(far)
    part, near, *far = call(
        functools.partial(middle_kernel, levels, n_far),
        "middle",
        [me, remote, pairs.T],
        [near, *far, state, stiff1, asm0, asm1, geo, mass, weight, bins, *ops, selt],
        [shape(192, 512), shape(n_near, K, 256)] + [shape(K, 256)] * n_far,
        [VM((384, 128), F32)] * 4,
    )
    near, late, early = spread(near), far[:2], swap(far[2:], 2)
    sums, *late = pl.pallas_call(
        functools.partial(merge_kernel, nz, len(early) + len(late)),
        out_shape=[shape(nz, 3, 128)] + [shape(K, 256)] * len(late),
        grid=(1,),
        in_specs=[pl.BlockSpec((n_near, K, 128), lambda i: (0, 0, 1))] + [ANY] * (len(early) + len(late)),
        out_specs=[pl.BlockSpec((nz, 3, 128), lambda i: (0, 0, 0))] + [ANY] * len(late),
        input_output_aliases={1 + len(early) + i: 1 + i for i in range(len(late))},
        compiler_params=PARAMS,
        name="merge",
    )(near, *early, *late)
    sums = lax.all_to_all(sums, "z", 0, 0, tiled=True)
    far = swap(late) + early
    (final,) = call(
        functools.partial(last_kernel, levels, n_far),
        "last",
        [me, remote],
        [near, *far, part, mass, selt],
        [shape(E, 1536)],
        [VM((384, 128), F32)] * 2,
    )
    points = nz * n_near * E * 512
    return final, jnp.sum(sums, axis=0) * (1.0 / math.sqrt(points / NBIN))


def solution(mesh):
    gx, gy = mesh.shape["gx"], mesh.shape["gy"]
    nx = 4 if gx >= 16 else 2
    sizes = (gx // nx, nx, gy // 2, 2)
    names = ("z", "x", "y", "c")
    inner = Mesh(mesh.devices.reshape(sizes), names)
    rows = P(names, None)
    return jax.shard_map(
        functools.partial(on_device, sizes),
        mesh=inner,
        in_specs=(rows,) * 7,
        out_specs=(rows, P()),
        check_vma=False,
    )
```

```python
import functools
import math

import jax
import jax.numpy as jnp
import numpy as np
from jax import lax
from jax.experimental import pallas as pl
from jax.experimental.pallas import tpu as pltpu
from jax.sharding import Mesh
from jax.sharding import PartitionSpec as P

NBIN = 128
STEP = 0.00015
E = 64
K = 24
F32 = jnp.float32
BF16 = jnp.bfloat16
VM = pltpu.VMEM


def cheb():
    m = np.arange(8)
    x = np.cos(np.pi * m / 7.0)
    c = np.where((m == 0) | (m == 7), 2.0, 1.0)
    sign = np.where((m[:, None] + m[None, :]) % 2 == 0, 1.0, -1.0)
    same = m[:, None] == m[None, :]
    gap = np.where(same, 1.0, x[:, None] - x[None, :])
    off = np.where(same, 0.0, c[:, None] / c[None, :] * sign / gap)
    return off - np.diag(off.sum(axis=1))


def split_const(a):
    hi = a.astype(np.float32).astype(jnp.bfloat16)
    lo = (a - hi.astype(np.float64)).astype(np.float32).astype(jnp.bfloat16)
    return hi, lo


def constants():
    d = cheb()
    last = np.kron(np.eye(16), d.T)
    middle = np.kron(np.kron(np.eye(2), d.T), np.eye(8))
    fh, fl = split_const(np.concatenate([last, middle], axis=1))
    forward = np.concatenate([fh, fh, fl], axis=0)
    bh, bl = split_const(np.concatenate([last.T, middle.T], axis=0))
    back = np.concatenate([bh, bl], axis=1)
    rows = []
    for mat in (d, d.T):
        for cross in (0, 1):
            for out in range(4):
                for src in range(4):
                    low = mat[2 * out, 2 * src + cross]
                    high = mat[2 * out + 1, 2 * src + 1 - cross]
                    rows.append(np.repeat([low, high], 64))
    coef = np.stack(rows).astype(np.float32)
    p = np.arange(64)
    u, l = p // 8, p % 8
    targets = np.concatenate(
        [p, 448 + p, u * 64 + l, u * 64 + 56 + l, u * 64 + l * 8, u * 64 + l * 8 + 7]
    )
    sel = np.arange(512)[:, None] == targets[None, :]
    sel = sel.astype(np.float32).astype(jnp.bfloat16)
    return forward, back, coef, sel, np.ascontiguousarray(sel.T)


def split(x):
    hi = x.astype(BF16)
    return hi, (x - hi.astype(F32)).astype(BF16)


def dot(a, b):
    return lax.dot_general(a, b, (((1,), (0,)), ((), ())), preferred_element_type=F32)


def thrice(x):
    return jnp.concatenate([x, x, x], axis=0)


def stiffness(x, geo, fwd, back, coef):
    quads = [x[:, 128 * q : 128 * q + 128] for q in range(4)]
    rows = jnp.concatenate(quads, axis=0)
    hi, lo = split(rows)
    grads = dot(jnp.concatenate([hi, lo], axis=1), fwd[0:256, :]) + dot(hi, fwd[256:384, :])
    scaled = []
    for q in range(4):
        metric = jnp.concatenate(
            [
                geo[:, 1024 + 128 * q : 1152 + 128 * q],
                geo[:, 512 + 128 * q : 640 + 128 * q],
            ],
            axis=1,
        )
        scaled.append(grads[192 * q : 192 * q + 192] * thrice(metric))
    hi, lo = split(jnp.concatenate(scaled, axis=0))
    both = dot(hi, back[...])
    lanes = both[:, :128] + both[:, 128:] + dot(lo, back[:, 0:128])
    out = []
    for part in range(6):
        lo_row = 32 * part
        e0 = lo_row % 64
        xs = [q[lo_row : lo_row + 32] for q in quads]
        rolled = [pltpu.roll(v, 64, 1) for v in xs]
        mids = []
        for o in range(4):
            acc = None
            for s in range(4):
                r = 4 * o + s
                term = coef[r : r + 1, :] * xs[s] + coef[16 + r : 17 + r, :] * rolled[s]
                acc = term if acc is None else acc + term
            mids.append(acc * geo[e0 : e0 + 32, 128 * o : 128 * o + 128])
        rolled = [pltpu.roll(v, 64, 1) for v in mids]
        cols = []
        for o in range(4):
            base = 192 * o + lo_row
            acc = lanes[base : base + 32]
            for s in range(4):
                r = 32 + 4 * o + s
                acc = acc + coef[r : r + 1, :] * mids[s] + coef[16 + r : 17 + r, :] * rolled[s]
            cols.append(acc)
        out.append(jnp.concatenate(cols, axis=1))
    return jnp.concatenate(out, axis=0)


def store_panels(stiff, extra, sel, pm):
    hi, lo = split(stiff)
    stack = [hi, lo]
    if extra is not None:
        weight, bins = extra
        stack += [*split(weight), bins.astype(BF16)]
    got = dot(jnp.concatenate(stack, axis=0), sel[...])
    face = got[0:192] + got[192:384]
    if extra is not None:
        wface = got[384:448] + got[448:512]
        bface = got[512:576]
    zero = jnp.zeros((E, 64), F32)
    for f in range(6):
        cut = slice(64 * f, 64 * f + 64)
        c0, c1, c2 = (face[64 * c : 64 * c + 64, cut] for c in range(3))
        third = zero if extra is None else wface[:, cut]
        pm[0][pl.ds(f, E, stride=6), :] = jnp.concatenate([c0, c1], axis=1)
        pm[1][pl.ds(f, E, stride=6), :] = jnp.concatenate([c2, third], axis=1)
        if extra is not None:
            pm[2][pl.ds(f, E, stride=6), :] = jnp.concatenate([bface[:, cut], zero], axis=1)


def send_rows(remote, me, levels, pm, out_near, out_far):
    for r, (kind, where) in enumerate(levels):
        for k in range(K):
            face = remote[r, k]
            for i, block in enumerate(pm):
                row, lanes = block[pl.ds(face, 1), :], slice(128 * i, 128 * i + 128)
                if kind == "near":
                    out_near[me[0] ^ where, k : k + 1, lanes] = row
                else:
                    out_far[where][k : k + 1, lanes] = row


def take_rows(remote, me, levels, near, far, asm):
    for r, (kind, where) in enumerate(levels):
        for k in range(K):
            face = remote[r, k]
            for i, block in enumerate(asm):
                lanes = slice(128 * i, 128 * i + 128)
                if kind == "near":
                    row = near[me[0] ^ where, k : k + 1, lanes]
                else:
                    row = far[where][k : k + 1, lanes]
                block[pl.ds(face, 1), :] = row


def pair_rows(pairs, pm, asm):
    for i in range(pairs.shape[1]):
        a, b = pairs[0, i], pairs[1, i]
        for source, block in zip(pm, asm):
            block[pl.ds(b, 1), :] = source[pl.ds(a, 1), :]
            block[pl.ds(a, 1), :] = source[pl.ds(b, 1), :]


def lift(asm, selt):
    faces = []
    for f in range(6):
        one = asm[0][pl.ds(f, E, stride=6), :]
        two = asm[1][pl.ds(f, E, stride=6), :]
        faces.append(jnp.concatenate([one[:, 0:64], one[:, 64:128], two[:, 0:64]], axis=0))
    hi, lo = split(jnp.concatenate(faces, axis=1))
    got = dot(jnp.concatenate([hi, lo], axis=0), selt[...])
    return got[0:192] + got[192:384]


def bin_dot(ws, bins):
    groups = bins.shape[0] // 8
    left, right = [], []
    for g in range(groups):
        cut = slice(8 * g, 8 * g + 8)
        b = bins[cut]
        upper, lower = b >> 5, b & 31
        masks = [upper == u for u in range(4)]
        rows = [jnp.where(m, w[cut], 0.0) for w in ws for m in masks]
        left.append(jnp.concatenate(rows, axis=0))
        ones = [jnp.where(lower == v, 1.0, 0.0) for v in range(32)]
        right.append(jnp.concatenate(ones, axis=0).astype(BF16))
    hi, lo = split(jnp.concatenate(left, axis=1))
    return lax.dot_general(
        jnp.concatenate([hi, lo], axis=0),
        jnp.concatenate(right, axis=1),
        (((1,), (1,)), ((), ())),
        preferred_element_type=F32,
    )


def bin_finish(acc):
    row = lax.broadcasted_iota(jnp.int32, (192, 256), 0)
    col = lax.broadcasted_iota(jnp.int32, (192, 256), 1)
    acc = jnp.where((row & 7) == (col & 7), acc, 0.0)
    summed = jnp.sum(acc.reshape(24, 8, 256), axis=1)
    r = lax.broadcasted_iota(jnp.int32, (256, 128), 0)
    c = lax.broadcasted_iota(jnp.int32, (256, 128), 1)
    put = jnp.where((r >> 3) + 64 == c, 1.0, 0.0)
    summed = summed[0:12] + summed[12:24]
    return jnp.dot(summed, put, precision=lax.Precision.HIGHEST, preferred_element_type=F32)


def first_kernel(levels, me, remote, pairs, state, geo, mass, weight, bins, fwd, back, coef, sel, *outs):
    stiff_out, asm0, asm1, out_near, *rest = outs
    out_far, pm = rest[:-3], rest[-3:]
    x = jnp.concatenate([state[:, 512 * c : 512 * c + 512] for c in range(3)], axis=0)
    stiff = stiffness(x, geo, fwd, back, coef)
    stiff_out[...] = stiff
    shares = (-STEP) * weight[...] * mass[...]
    store_panels(stiff, (shares, bins[...].astype(F32)), sel, pm)
    send_rows(remote, me, levels, pm, out_near, out_far)
    asm0[...] = jnp.zeros_like(asm0)
    asm1[...] = jnp.zeros_like(asm1)
    pair_rows(pairs, pm, (asm0, asm1))


def middle_kernel(levels, n_far, me, remote, pairs, *refs):
    near, far = refs[0], refs[1 : 1 + n_far]
    rest = refs[1 + n_far :]
    state, stiff1, asm0, asm1, geo, mass, weight, bins, fwd, back, coef, sel, selt = rest[:13]
    part_out, out_near = rest[13], rest[14]
    out_far = rest[15 : 15 + n_far]
    asm, pm = rest[15 + n_far : 17 + n_far], rest[17 + n_far :]
    asm[0][...] = asm0[...]
    asm[1][...] = asm1[...]
    take_rows(remote, me, levels, near, far, asm)
    scale = thrice(STEP * mass[...])
    x = jnp.concatenate([state[:, 512 * c : 512 * c + 512] for c in range(3)], axis=0)
    x = x - scale * (stiff1[...] + lift(asm, selt))
    stiff = stiffness(x, geo, fwd, back, coef)
    store_panels(stiff, None, sel, pm)
    send_rows(remote, me, levels, pm, out_near, out_far)
    asm[0][...] = jnp.zeros_like(asm0)
    asm[1][...] = jnp.zeros_like(asm1)
    pair_rows(pairs, pm, asm)
    part = x - scale * (stiff + lift(asm, selt))
    part_out[...] = part
    total = x + part
    w = weight[...]
    acc = bin_dot([w * total[64 * c : 64 * c + 64] for c in range(3)], bins[...])
    lane = lax.broadcasted_iota(jnp.int32, (K, 128), 1)
    for r, (kind, where) in enumerate(levels):
        if kind == "near":
            j = me[0] ^ where
            got, sent = (lambda a, b: near[j, :, a:b]), (lambda a, b: out_near[j, :, a:b])
        else:
            got = lambda a, b, ref=far[where]: ref[:, a:b]
            sent = lambda a, b, ref=out_far[where]: ref[:, a:b]
        high, bin_low = got(128, 256), got(256, 384)
        share = jnp.where(lane < 64, pltpu.roll(high, 64, 1), high)
        label = jnp.where(lane < 64, bin_low, pltpu.roll(bin_low, 64, 1)).astype(jnp.int32)
        first = sent(0, 128) * share
        second = jnp.where(lane < 64, sent(128, 256) * share, 0.0)
        fields = [jnp.where(lane < 64, first, 0.0), jnp.where(lane < 64, 0.0, first), second]
        acc = acc + bin_dot(fields, label)
    sums = bin_finish(acc)
    for j in range(out_near.shape[0]):
        out_near[j, 0:12, 192:256] = sums[:, 64:128]


def merge_kernel(n_in, near, *refs):
    out = refs[n_in]
    sums = jnp.sum(near[:, :, :], axis=0)
    row = lax.broadcasted_iota(jnp.int32, (K, 128), 0)
    col = lax.broadcasted_iota(jnp.int32, (K, 128), 1)
    r = lax.broadcasted_iota(jnp.int32, (128, 128), 0)
    c = lax.broadcasted_iota(jnp.int32, (128, 128), 1)
    spread = jnp.where((r >= 64) & (r < 96) & ((c & 31) == r - 64), 1.0, 0.0)
    sums = jnp.where((row < 12) & (col >= 64) & (col < 96), sums, 0.0)
    full = jnp.dot(sums, spread, precision=lax.Precision.HIGHEST, preferred_element_type=F32)
    full = jnp.where((row & 3) == (col >> 5), full, 0.0)
    done = jnp.concatenate([jnp.sum(full[4 * i : 4 * i + 4], axis=0, keepdims=True) for i in range(3)], axis=0)
    for j in range(out.shape[0]):
        out[j] = done


def last_kernel(levels, n_far, me, remote, *refs):
    near, far = refs[0], refs[1 : 1 + n_far]
    part, mass, selt, out, *asm = refs[1 + n_far :]
    for block in asm:
        block[...] = jnp.zeros_like(block)
    take_rows(remote, me, levels, near, far, asm)
    moved = part[...] - thrice(STEP * mass[...]) * lift(asm, selt)
    for c in range(3):
        out[:, 512 * c : 512 * c + 512] = moved[64 * c : 64 * c + 64]


SMEM = pl.BlockSpec(memory_space=pltpu.SMEM)
ANY = pl.BlockSpec(memory_space=pl.ANY)
PARAMS = pltpu.CompilerParams(vmem_limit_bytes=56 * 1024 * 1024)


def whole(a):
    return pl.BlockSpec(a.shape, lambda i, n=len(a.shape): (0,) * n)


def call(kernel, name, scalars, arrays, outs, scratch):
    return pl.pallas_call(
        kernel,
        out_shape=outs,
        grid=(1,),
        in_specs=[SMEM] * len(scalars) + [whole(a) for a in arrays],
        out_specs=[whole(a) for a in outs],
        scratch_shapes=scratch,
        compiler_params=PARAMS,
        name=name,
    )(*scalars, *arrays)


def on_device(sizes, state, geo, mass, weight, bins, pairs, remote):
    nz, nx, ny, nc = sizes
    group = ("x", "y", "c")
    n_near = nx * ny * nc
    log = lambda n: n.bit_length() - 1
    n_far = log(nz)
    levels = [("near", ny * nc * 2**b) for b in range(log(nx))]
    levels += [("far", n_far - 1 - b) for b in range(n_far)]
    levels += [("near", 2**b) for b in range(log(ny * nc))]
    fwd, back, coef, sel, selt = (jnp.asarray(a) for a in constants())
    me = lax.axis_index(group).astype(jnp.int32).reshape(1)
    shape = lambda *dims: jax.ShapeDtypeStruct(dims, F32)

    def swap(far, first=0):
        masks = [2 ** (n_far - 1 - first - i) for i in range(len(far))]
        return [lax.ppermute(v, "z", [(s, s ^ m) for s in range(nz)]) for v, m in zip(far, masks)]

    def spread(near):
        return lax.all_to_all(near, group, 0, 0, tiled=True)

    ops = [fwd, back, coef, sel]
    stiff1, asm0, asm1, near, *far = call(
        functools.partial(first_kernel, levels),
        "first",
        [me, remote, pairs.T],
        [state, geo, mass, weight, bins, *ops],
        [shape(192, 512), shape(384, 128), shape(384, 128), shape(n_near, K, 384)]
        + [shape(K, 384)] * n_far,
        [VM((384, 128), F32)] * 3,
    )
    near, far = spread(near), swap(far)
    part, near, *far = call(
        functools.partial(middle_kernel, levels, n_far),
        "middle",
        [me, remote, pairs.T],
        [near, *far, state, stiff1, asm0, asm1, geo, mass, weight, bins, *ops, selt],
        [shape(192, 512), shape(n_near, K, 256)] + [shape(K, 256)] * n_far,
        [VM((384, 128), F32)] * 4,
    )
    near, far = spread(near), swap(far)
    sums = pl.pallas_call(
        functools.partial(merge_kernel, n_far),
        out_shape=shape(nz, 3, 128),
        grid=(1,),
        in_specs=[pl.BlockSpec((n_near, K, 128), lambda i: (0, 0, 1))] + [ANY] * n_far,
        out_specs=pl.BlockSpec((nz, 3, 128), lambda i: (0, 0, 0)),
        compiler_params=PARAMS,
        name="merge",
    )(near, *far)
    sums = lax.all_to_all(sums, "z", 0, 0, tiled=True)
    (final,) = call(
        functools.partial(last_kernel, levels, n_far),
        "last",
        [me, remote],
        [near, *far, part, mass, selt],
        [shape(E, 1536)],
        [VM((384, 128), F32)] * 2,
    )
    points = nz * n_near * E * 512
    return final, jnp.sum(sums, axis=0) * (1.0 / math.sqrt(points / NBIN))


def solution(mesh):
    gx, gy = mesh.shape["gx"], mesh.shape["gy"]
    nx = 4 if gx >= 16 else 2
    sizes = (gx // nx, nx, gy // 2, 2)
    names = ("z", "x", "y", "c")
    inner = Mesh(mesh.devices.reshape(sizes), names)
    rows = P(names, None)
    return jax.shard_map(
        functools.partial(on_device, sizes),
        mesh=inner,
        in_specs=(rows,) * 7,
        out_specs=(rows, P()),
        check_vma=False,
    )
```

```python
import functools
import math

import jax
import jax.numpy as jnp
import numpy as np
from jax import lax
from jax.experimental import pallas as pl
from jax.experimental.pallas import tpu as pltpu
from jax.sharding import Mesh
from jax.sharding import PartitionSpec as P

NBIN = 128
STEP = 0.00015
E = 64
K = 24
F32 = jnp.float32
BF16 = jnp.bfloat16
VM = pltpu.VMEM


def cheb():
    m = np.arange(8)
    x = np.cos(np.pi * m / 7.0)
    c = np.where((m == 0) | (m == 7), 2.0, 1.0)
    sign = np.where((m[:, None] + m[None, :]) % 2 == 0, 1.0, -1.0)
    same = m[:, None] == m[None, :]
    gap = np.where(same, 1.0, x[:, None] - x[None, :])
    off = np.where(same, 0.0, c[:, None] / c[None, :] * sign / gap)
    return off - np.diag(off.sum(axis=1))


def split_const(a):
    hi = a.astype(np.float32).astype(jnp.bfloat16)
    lo = (a - hi.astype(np.float64)).astype(np.float32).astype(jnp.bfloat16)
    return hi, lo


def constants():
    d = cheb()
    last = np.kron(np.eye(16), d.T)
    middle = np.kron(np.kron(np.eye(2), d.T), np.eye(8))
    fh, fl = split_const(np.concatenate([last, middle], axis=1))
    forward = np.concatenate([fh, fh, fl], axis=0)
    bh, bl = split_const(np.concatenate([last.T, middle.T], axis=0))
    back = np.concatenate([bh, bl], axis=1)
    rows = []
    for mat in (d, d.T):
        for cross in (0, 1):
            for out in range(4):
                for src in range(4):
                    low = mat[2 * out, 2 * src + cross]
                    high = mat[2 * out + 1, 2 * src + 1 - cross]
                    rows.append(np.repeat([low, high], 64))
    coef = np.stack(rows).astype(np.float32)
    p = np.arange(64)
    u, l = p // 8, p % 8
    targets = np.concatenate(
        [p, 448 + p, u * 64 + l, u * 64 + 56 + l, u * 64 + l * 8, u * 64 + l * 8 + 7]
    )
    sel = np.arange(512)[:, None] == targets[None, :]
    sel = sel.astype(np.float32).astype(jnp.bfloat16)
    return forward, back, coef, sel, np.ascontiguousarray(sel.T)


def split(x):
    hi = x.astype(BF16)
    return hi, (x - hi.astype(F32)).astype(BF16)


def dot(a, b):
    return lax.dot_general(a, b, (((1,), (0,)), ((), ())), preferred_element_type=F32)


def thrice(x):
    return jnp.concatenate([x, x, x], axis=0)


def stiffness(x, geo, fwd, back, coef):
    quads = [x[:, 128 * q : 128 * q + 128] for q in range(4)]
    rows = jnp.concatenate(quads, axis=0)
    hi, lo = split(rows)
    grads = dot(jnp.concatenate([hi, lo], axis=1), fwd[0:256, :]) + dot(hi, fwd[256:384, :])
    scaled = []
    for q in range(4):
        metric = jnp.concatenate(
            [
                geo[:, 1024 + 128 * q : 1152 + 128 * q],
                geo[:, 512 + 128 * q : 640 + 128 * q],
            ],
            axis=1,
        )
        scaled.append(grads[192 * q : 192 * q + 192] * thrice(metric))
    hi, lo = split(jnp.concatenate(scaled, axis=0))
    both = dot(hi, back[...])
    lanes = both[:, :128] + both[:, 128:] + dot(lo, back[:, 0:128])
    out = []
    for part in range(6):
        lo_row = 32 * part
        e0 = lo_row % 64
        xs = [q[lo_row : lo_row + 32] for q in quads]
        rolled = [pltpu.roll(v, 64, 1) for v in xs]
        mids = []
        for o in range(4):
            acc = None
            for s in range(4):
                r = 4 * o + s
                term = coef[r : r + 1, :] * xs[s] + coef[16 + r : 17 + r, :] * rolled[s]
                acc = term if acc is None else acc + term
            mids.append(acc * geo[e0 : e0 + 32, 128 * o : 128 * o + 128])
        rolled = [pltpu.roll(v, 64, 1) for v in mids]
        cols = []
        for o in range(4):
            base = 192 * o + lo_row
            acc = lanes[base : base + 32]
            for s in range(4):
                r = 32 + 4 * o + s
                acc = acc + coef[r : r + 1, :] * mids[s] + coef[16 + r : 17 + r, :] * rolled[s]
            cols.append(acc)
        out.append(jnp.concatenate(cols, axis=1))
    return jnp.concatenate(out, axis=0)


def store_panels(stiff, extra, sel, pm):
    hi, lo = split(stiff)
    stack = [hi, lo]
    if extra is not None:
        weight, bins = extra
        stack += [*split(weight), bins.astype(BF16)]
    got = dot(jnp.concatenate(stack, axis=0), sel[...])
    face = got[0:192] + got[192:384]
    if extra is not None:
        wface = got[384:448] + got[448:512]
        bface = got[512:576]
    zero = jnp.zeros((E, 64), F32)
    for f in range(6):
        cut = slice(64 * f, 64 * f + 64)
        c0, c1, c2 = (face[64 * c : 64 * c + 64, cut] for c in range(3))
        third = zero if extra is None else wface[:, cut]
        pm[0][pl.ds(f, E, stride=6), :] = jnp.concatenate([c0, c1], axis=1)
        pm[1][pl.ds(f, E, stride=6), :] = jnp.concatenate([c2, third], axis=1)
        if extra is not None:
            pm[2][pl.ds(f, E, stride=6), :] = jnp.concatenate([bface[:, cut], zero], axis=1)


def send_rows(remote, me, levels, pm, out_near, out_far):
    for r, (kind, where) in enumerate(levels):
        for k in range(K):
            face = remote[r, k]
            for i, block in enumerate(pm):
                row, lanes = block[pl.ds(face, 1), :], slice(128 * i, 128 * i + 128)
                if kind == "near":
                    out_near[me[0] ^ where, k : k + 1, lanes] = row
                else:
                    out_far[where][k : k + 1, lanes] = row


def take_rows(remote, me, levels, near, far, asm):
    for r, (kind, where) in enumerate(levels):
        for k in range(K):
            face = remote[r, k]
            for i, block in enumerate(asm):
                lanes = slice(128 * i, 128 * i + 128)
                if kind == "near":
                    row = near[me[0] ^ where, k : k + 1, lanes]
                else:
                    row = far[where][k : k + 1, lanes]
                block[pl.ds(face, 1), :] = row


def pair_rows(pairs, pm, asm):
    for i in range(pairs.shape[1]):
        a, b = pairs[0, i], pairs[1, i]
        for source, block in zip(pm, asm):
            block[pl.ds(b, 1), :] = source[pl.ds(a, 1), :]
            block[pl.ds(a, 1), :] = source[pl.ds(b, 1), :]


def lift(asm, selt):
    faces = []
    for f in range(6):
        one = asm[0][pl.ds(f, E, stride=6), :]
        two = asm[1][pl.ds(f, E, stride=6), :]
        faces.append(jnp.concatenate([one[:, 0:64], one[:, 64:128], two[:, 0:64]], axis=0))
    hi, lo = split(jnp.concatenate(faces, axis=1))
    got = dot(jnp.concatenate([hi, lo], axis=0), selt[...])
    return got[0:192] + got[192:384]


def bin_dot(ws, bins):
    groups = bins.shape[0] // 8
    left, right = [], []
    for g in range(groups):
        cut = slice(8 * g, 8 * g + 8)
        b = bins[cut]
        upper, lower = b >> 5, b & 31
        masks = [upper == u for u in range(4)]
        rows = [jnp.where(m, w[cut], 0.0) for w in ws for m in masks]
        left.append(jnp.concatenate(rows, axis=0))
        ones = [jnp.where(lower == v, 1.0, 0.0) for v in range(32)]
        right.append(jnp.concatenate(ones, axis=0).astype(BF16))
    hi, lo = split(jnp.concatenate(left, axis=1))
    return lax.dot_general(
        jnp.concatenate([hi, lo], axis=0),
        jnp.concatenate(right, axis=1),
        (((1,), (1,)), ((), ())),
        preferred_element_type=F32,
    )


def bin_finish(acc):
    row = lax.broadcasted_iota(jnp.int32, (192, 256), 0)
    col = lax.broadcasted_iota(jnp.int32, (192, 256), 1)
    acc = jnp.where((row & 7) == (col & 7), acc, 0.0)
    summed = jnp.sum(acc.reshape(24, 8, 256), axis=1)
    r = lax.broadcasted_iota(jnp.int32, (256, 128), 0)
    c = lax.broadcasted_iota(jnp.int32, (256, 128), 1)
    put = jnp.where((r >> 3) + 64 == c, 1.0, 0.0)
    summed = summed[0:12] + summed[12:24]
    return jnp.dot(summed, put, precision=lax.Precision.HIGHEST, preferred_element_type=F32)


def first_kernel(levels, me, remote, pairs, state, geo, mass, weight, bins, fwd, back, coef, sel, *outs):
    stiff_out, asm0, asm1, out_near, *rest = outs
    out_far, pm = rest[:-3], rest[-3:]
    x = jnp.concatenate([state[:, 512 * c : 512 * c + 512] for c in range(3)], axis=0)
    stiff = stiffness(x, geo, fwd, back, coef)
    stiff_out[...] = stiff
    shares = (-STEP) * weight[...] * mass[...]
    store_panels(stiff, (shares, bins[...].astype(F32)), sel, pm)
    send_rows(remote, me, levels, pm, out_near, out_far)
    asm0[...] = jnp.zeros_like(asm0)
    asm1[...] = jnp.zeros_like(asm1)
    pair_rows(pairs, pm, (asm0, asm1))


def middle_kernel(levels, n_far, me, remote, pairs, *refs):
    near, far = refs[0], refs[1 : 1 + n_far]
    rest = refs[1 + n_far :]
    state, stiff1, asm0, asm1, geo, mass, weight, bins, fwd, back, coef, sel, selt = rest[:13]
    part_out, out_near = rest[13], rest[14]
    out_far = rest[15 : 15 + n_far]
    asm, pm = rest[15 + n_far : 17 + n_far], rest[17 + n_far :]
    asm[0][...] = asm0[...]
    asm[1][...] = asm1[...]
    take_rows(remote, me, levels, near, far, asm)
    scale = thrice(STEP * mass[...])
    x = jnp.concatenate([state[:, 512 * c : 512 * c + 512] for c in range(3)], axis=0)
    x = x - scale * (stiff1[...] + lift(asm, selt))
    stiff = stiffness(x, geo, fwd, back, coef)
    store_panels(stiff, None, sel, pm)
    send_rows(remote, me, levels, pm, out_near, out_far)
    asm[0][...] = jnp.zeros_like(asm0)
    asm[1][...] = jnp.zeros_like(asm1)
    pair_rows(pairs, pm, asm)
    part = x - scale * (stiff + lift(asm, selt))
    part_out[...] = part
    total = x + part
    w = weight[...]
    acc = bin_dot([w * total[64 * c : 64 * c + 64] for c in range(3)], bins[...])
    lane = lax.broadcasted_iota(jnp.int32, (K, 128), 1)
    for r, (kind, where) in enumerate(levels):
        if kind == "near":
            j = me[0] ^ where
            got, sent = (lambda a, b: near[j, :, a:b]), (lambda a, b: out_near[j, :, a:b])
        else:
            got = lambda a, b, ref=far[where]: ref[:, a:b]
            sent = lambda a, b, ref=out_far[where]: ref[:, a:b]
        high, bin_low = got(128, 256), got(256, 384)
        share = jnp.where(lane < 64, pltpu.roll(high, 64, 1), high)
        label = jnp.where(lane < 64, bin_low, pltpu.roll(bin_low, 64, 1)).astype(jnp.int32)
        first = sent(0, 128) * share
        second = jnp.where(lane < 64, sent(128, 256) * share, 0.0)
        fields = [jnp.where(lane < 64, first, 0.0), jnp.where(lane < 64, 0.0, first), second]
        acc = acc + bin_dot(fields, label)
    sums = bin_finish(acc)
    for j in range(out_near.shape[0]):
        out_near[j, 0:12, 192:256] = sums[:, 64:128]


def merge_kernel(copies, n_in, near, *refs):
    out = refs[n_in]
    sums = jnp.sum(near[:, :, :], axis=0)
    row = lax.broadcasted_iota(jnp.int32, (K, 128), 0)
    col = lax.broadcasted_iota(jnp.int32, (K, 128), 1)
    r = lax.broadcasted_iota(jnp.int32, (128, 128), 0)
    c = lax.broadcasted_iota(jnp.int32, (128, 128), 1)
    spread = jnp.where((r >= 64) & (r < 96) & ((c & 31) == r - 64), 1.0, 0.0)
    sums = jnp.where((row < 12) & (col >= 64) & (col < 96), sums, 0.0)
    full = jnp.dot(sums, spread, precision=lax.Precision.HIGHEST, preferred_element_type=F32)
    full = jnp.where((row & 3) == (col >> 5), full, 0.0)
    done = jnp.concatenate([jnp.sum(full[4 * i : 4 * i + 4], axis=0, keepdims=True) for i in range(3)], axis=0)
    for j in range(copies):
        out[j] = done


def last_kernel(levels, n_far, me, remote, *refs):
    near, far = refs[0], refs[1 : 1 + n_far]
    part, mass, selt, out, *asm = refs[1 + n_far :]
    for block in asm:
        block[...] = jnp.zeros_like(block)
    take_rows(remote, me, levels, near, far, asm)
    moved = part[...] - thrice(STEP * mass[...]) * lift(asm, selt)
    for c in range(3):
        out[:, 512 * c : 512 * c + 512] = moved[64 * c : 64 * c + 64]


SMEM = pl.BlockSpec(memory_space=pltpu.SMEM)
ANY = pl.BlockSpec(memory_space=pl.ANY)
PARAMS = pltpu.CompilerParams(vmem_limit_bytes=56 * 1024 * 1024)


def whole(a):
    return pl.BlockSpec(a.shape, lambda i, n=len(a.shape): (0,) * n)


def call(kernel, name, scalars, arrays, outs, scratch):
    return pl.pallas_call(
        kernel,
        out_shape=outs,
        grid=(1,),
        in_specs=[SMEM] * len(scalars) + [whole(a) for a in arrays],
        out_specs=[whole(a) for a in outs],
        scratch_shapes=scratch,
        compiler_params=PARAMS,
        name=name,
    )(*scalars, *arrays)


def hold_kernel(*refs):
    pass


def hold(arrays):
    n = len(arrays)
    return pl.pallas_call(
        hold_kernel,
        out_shape=[jax.ShapeDtypeStruct(a.shape, a.dtype) for a in arrays],
        in_specs=[ANY] * n,
        out_specs=[ANY] * n,
        input_output_aliases={i: i for i in range(n)},
        cost_estimate=pl.CostEstimate(flops=40_000_000_000, bytes_accessed=0, transcendentals=0),
        name="hold",
    )(*arrays)


def on_device(sizes, state, geo, mass, weight, bins, pairs, remote):
    nz, nx, ny, nc = sizes
    group = ("x", "y", "c")
    n_near = nx * ny * nc
    log = lambda n: n.bit_length() - 1
    n_far = log(nz)
    levels = [("near", ny * nc * 2**b) for b in range(log(nx))]
    levels += [("far", n_far - 1 - b) for b in range(n_far)]
    levels += [("near", 2**b) for b in range(log(ny * nc))]
    fwd, back, coef, sel, selt = (jnp.asarray(a) for a in constants())
    me = lax.axis_index(group).astype(jnp.int32).reshape(1)
    shape = lambda *dims: jax.ShapeDtypeStruct(dims, F32)

    def swap(far, first=0):
        masks = [2 ** (n_far - 1 - first - i) for i in range(len(far))]
        return [lax.ppermute(v, "z", [(s, s ^ m) for s in range(nz)]) for v, m in zip(far, masks)]

    def spread(near):
        return lax.all_to_all(near, group, 0, 0, tiled=True)

    ops = [fwd, back, coef, sel]
    stiff1, asm0, asm1, near, *far = call(
        functools.partial(first_kernel, levels),
        "first",
        [me, remote, pairs.T],
        [state, geo, mass, weight, bins, *ops],
        [shape(192, 512), shape(384, 128), shape(384, 128), shape(n_near, K, 384)]
        + [shape(K, 384)] * n_far,
        [VM((384, 128), F32)] * 3,
    )
    near, far = spread(near), swap(far)
    far = [*hold(far[:1]), *far[1:]]
    part, near, *far = call(
        functools.partial(middle_kernel, levels, n_far),
        "middle",
        [me, remote, pairs.T],
        [near, *far, state, stiff1, asm0, asm1, geo, mass, weight, bins, *ops, selt],
        [shape(192, 512), shape(n_near, K, 256)] + [shape(K, 256)] * n_far,
        [VM((384, 128), F32)] * 4,
    )
    near, late = spread(near), far[2:]
    sums, *late = pl.pallas_call(
        functools.partial(merge_kernel, nz, len(late)),
        out_shape=[shape(nz, 3, 128)] + [shape(K, 256)] * len(late),
        grid=(1,),
        in_specs=[pl.BlockSpec((n_near, K, 128), lambda i: (0, 0, 1))] + [ANY] * len(late),
        out_specs=[pl.BlockSpec((nz, 3, 128), lambda i: (0, 0, 0))] + [ANY] * len(late),
        input_output_aliases={1 + i: 1 + i for i in range(len(late))},
        compiler_params=PARAMS,
        name="merge",
    )(near, *late)
    sums = lax.all_to_all(sums, "z", 0, 0, tiled=True)
    far = [*hold(swap(far[:2])), *swap(late, 2)]
    (final,) = call(
        functools.partial(last_kernel, levels, n_far),
        "last",
        [me, remote],
        [near, *far, part, mass, selt],
        [shape(E, 1536)],
        [VM((384, 128), F32)] * 2,
    )
    points = nz * n_near * E * 512
    return final, jnp.sum(sums, axis=0) * (1.0 / math.sqrt(points / NBIN))


def solution(mesh):
    gx, gy = mesh.shape["gx"], mesh.shape["gy"]
    nx = 4 if gx >= 16 else 2
    sizes = (gx // nx, nx, gy // 2, 2)
    names = ("z", "x", "y", "c")
    inner = Mesh(mesh.devices.reshape(sizes), names)
    rows = P(names, None)
    return jax.shard_map(
        functools.partial(on_device, sizes),
        mesh=inner,
        in_specs=(rows,) * 7,
        out_specs=(rows, P()),
        check_vma=False,
    )
```

```python
import functools
import math

import jax
import jax.numpy as jnp
import numpy as np
from jax import lax
from jax.experimental import pallas as pl
from jax.experimental.pallas import tpu as pltpu
from jax.sharding import Mesh
from jax.sharding import PartitionSpec as P

NBIN = 128
STEP = 0.00015
E = 64
K = 24
F32 = jnp.float32
BF16 = jnp.bfloat16
VM = pltpu.VMEM


def cheb():
    m = np.arange(8)
    x = np.cos(np.pi * m / 7.0)
    c = np.where((m == 0) | (m == 7), 2.0, 1.0)
    sign = np.where((m[:, None] + m[None, :]) % 2 == 0, 1.0, -1.0)
    same = m[:, None] == m[None, :]
    gap = np.where(same, 1.0, x[:, None] - x[None, :])
    off = np.where(same, 0.0, c[:, None] / c[None, :] * sign / gap)
    return off - np.diag(off.sum(axis=1))


def split_const(a):
    hi = a.astype(np.float32).astype(jnp.bfloat16)
    lo = (a - hi.astype(np.float64)).astype(np.float32).astype(jnp.bfloat16)
    return hi, lo


def constants():
    d = cheb()
    last = np.kron(np.eye(16), d.T)
    middle = np.kron(np.kron(np.eye(2), d.T), np.eye(8))
    fh, fl = split_const(np.concatenate([last, middle], axis=1))
    forward = np.concatenate([fh, fh, fl], axis=0)
    bh, bl = split_const(np.concatenate([last.T, middle.T], axis=0))
    back = np.concatenate([bh, bl], axis=1)
    rows = []
    for mat in (d, d.T):
        for cross in (0, 1):
            for out in range(4):
                for src in range(4):
                    low = mat[2 * out, 2 * src + cross]
                    high = mat[2 * out + 1, 2 * src + 1 - cross]
                    rows.append(np.repeat([low, high], 64))
    coef = np.stack(rows).astype(np.float32)
    p = np.arange(64)
    u, l = p // 8, p % 8
    targets = np.concatenate(
        [p, 448 + p, u * 64 + l, u * 64 + 56 + l, u * 64 + l * 8, u * 64 + l * 8 + 7]
    )
    sel = np.arange(512)[:, None] == targets[None, :]
    sel = sel.astype(np.float32).astype(jnp.bfloat16)
    return forward, back, coef, sel, np.ascontiguousarray(sel.T)


def split(x):
    hi = x.astype(BF16)
    return hi, (x - hi.astype(F32)).astype(BF16)


def dot(a, b):
    return lax.dot_general(a, b, (((1,), (0,)), ((), ())), preferred_element_type=F32)


def thrice(x):
    return jnp.concatenate([x, x, x], axis=0)


def stiffness(x, geo, fwd, back, coef):
    quads = [x[:, 128 * q : 128 * q + 128] for q in range(4)]
    rows = jnp.concatenate(quads, axis=0)
    hi, lo = split(rows)
    grads = dot(jnp.concatenate([hi, lo], axis=1), fwd[0:256, :]) + dot(hi, fwd[256:384, :])
    scaled = []
    for q in range(4):
        metric = jnp.concatenate(
            [
                geo[:, 1024 + 128 * q : 1152 + 128 * q],
                geo[:, 512 + 128 * q : 640 + 128 * q],
            ],
            axis=1,
        )
        scaled.append(grads[192 * q : 192 * q + 192] * thrice(metric))
    hi, lo = split(jnp.concatenate(scaled, axis=0))
    both = dot(hi, back[...])
    lanes = both[:, :128] + both[:, 128:] + dot(lo, back[:, 0:128])
    out = []
    for part in range(6):
        lo_row = 32 * part
        e0 = lo_row % 64
        xs = [q[lo_row : lo_row + 32] for q in quads]
        rolled = [pltpu.roll(v, 64, 1) for v in xs]
        mids = []
        for o in range(4):
            acc = None
            for s in range(4):
                r = 4 * o + s
                term = coef[r : r + 1, :] * xs[s] + coef[16 + r : 17 + r, :] * rolled[s]
                acc = term if acc is None else acc + term
            mids.append(acc * geo[e0 : e0 + 32, 128 * o : 128 * o + 128])
        rolled = [pltpu.roll(v, 64, 1) for v in mids]
        cols = []
        for o in range(4):
            base = 192 * o + lo_row
            acc = lanes[base : base + 32]
            for s in range(4):
                r = 32 + 4 * o + s
                acc = acc + coef[r : r + 1, :] * mids[s] + coef[16 + r : 17 + r, :] * rolled[s]
            cols.append(acc)
        out.append(jnp.concatenate(cols, axis=1))
    return jnp.concatenate(out, axis=0)


def store_panels(stiff, extra, sel, pm):
    hi, lo = split(stiff)
    stack = [hi, lo]
    if extra is not None:
        weight, bins = extra
        stack += [*split(weight), bins.astype(BF16)]
    got = dot(jnp.concatenate(stack, axis=0), sel[...])
    face = got[0:192] + got[192:384]
    if extra is not None:
        wface = got[384:448] + got[448:512]
        bface = got[512:576]
    zero = jnp.zeros((E, 64), F32)
    for f in range(6):
        cut = slice(64 * f, 64 * f + 64)
        c0, c1, c2 = (face[64 * c : 64 * c + 64, cut] for c in range(3))
        third = zero if extra is None else wface[:, cut]
        pm[0][pl.ds(f, E, stride=6), :] = jnp.concatenate([c0, c1], axis=1)
        pm[1][pl.ds(f, E, stride=6), :] = jnp.concatenate([c2, third], axis=1)
        if extra is not None:
            pm[2][pl.ds(f, E, stride=6), :] = jnp.concatenate([bface[:, cut], zero], axis=1)


def send_rows(remote, me, levels, pm, out_near, out_far):
    for r, (kind, where) in enumerate(levels):
        for k in range(K):
            face = remote[r, k]
            for i, block in enumerate(pm):
                row, lanes = block[pl.ds(face, 1), :], slice(128 * i, 128 * i + 128)
                if kind == "near":
                    out_near[me[0] ^ where, k : k + 1, lanes] = row
                else:
                    out_far[where][k : k + 1, lanes] = row


def take_rows(remote, me, levels, near, far, asm):
    for r, (kind, where) in enumerate(levels):
        for k in range(K):
            face = remote[r, k]
            for i, block in enumerate(asm):
                lanes = slice(128 * i, 128 * i + 128)
                if kind == "near":
                    row = near[me[0] ^ where, k : k + 1, lanes]
                else:
                    row = far[where][k : k + 1, lanes]
                block[pl.ds(face, 1), :] = row


def pair_rows(pairs, pm, asm):
    for i in range(pairs.shape[1]):
        a, b = pairs[0, i], pairs[1, i]
        for source, block in zip(pm, asm):
            block[pl.ds(b, 1), :] = source[pl.ds(a, 1), :]
            block[pl.ds(a, 1), :] = source[pl.ds(b, 1), :]


def lift(asm, selt):
    faces = []
    for f in range(6):
        one = asm[0][pl.ds(f, E, stride=6), :]
        two = asm[1][pl.ds(f, E, stride=6), :]
        faces.append(jnp.concatenate([one[:, 0:64], one[:, 64:128], two[:, 0:64]], axis=0))
    hi, lo = split(jnp.concatenate(faces, axis=1))
    got = dot(jnp.concatenate([hi, lo], axis=0), selt[...])
    return got[0:192] + got[192:384]


def bin_dot(ws, bins):
    groups = bins.shape[0] // 8
    left, right = [], []
    for g in range(groups):
        cut = slice(8 * g, 8 * g + 8)
        b = bins[cut]
        upper, lower = b >> 5, b & 31
        masks = [upper == u for u in range(4)]
        rows = [jnp.where(m, w[cut], 0.0) for w in ws for m in masks]
        left.append(jnp.concatenate(rows, axis=0))
        ones = [jnp.where(lower == v, 1.0, 0.0) for v in range(32)]
        right.append(jnp.concatenate(ones, axis=0).astype(BF16))
    hi, lo = split(jnp.concatenate(left, axis=1))
    return lax.dot_general(
        jnp.concatenate([hi, lo], axis=0),
        jnp.concatenate(right, axis=1),
        (((1,), (1,)), ((), ())),
        preferred_element_type=F32,
    )


def bin_finish(acc):
    row = lax.broadcasted_iota(jnp.int32, (192, 256), 0)
    col = lax.broadcasted_iota(jnp.int32, (192, 256), 1)
    acc = jnp.where((row & 7) == (col & 7), acc, 0.0)
    summed = jnp.sum(acc.reshape(24, 8, 256), axis=1)
    r = lax.broadcasted_iota(jnp.int32, (256, 128), 0)
    c = lax.broadcasted_iota(jnp.int32, (256, 128), 1)
    put = jnp.where((r >> 3) + 64 == c, 1.0, 0.0)
    summed = summed[0:12] + summed[12:24]
    return jnp.dot(summed, put, precision=lax.Precision.HIGHEST, preferred_element_type=F32)


def first_kernel(levels, me, remote, pairs, state, geo, mass, weight, bins, fwd, back, coef, sel, *outs):
    stiff_out, asm0, asm1, out_near, *rest = outs
    out_far, pm = rest[:-3], rest[-3:]
    x = jnp.concatenate([state[:, 512 * c : 512 * c + 512] for c in range(3)], axis=0)
    stiff = stiffness(x, geo, fwd, back, coef)
    stiff_out[...] = stiff
    shares = (-STEP) * weight[...] * mass[...]
    store_panels(stiff, (shares, bins[...].astype(F32)), sel, pm)
    send_rows(remote, me, levels, pm, out_near, out_far)
    asm0[...] = jnp.zeros_like(asm0)
    asm1[...] = jnp.zeros_like(asm1)
    pair_rows(pairs, pm, (asm0, asm1))


def middle_kernel(levels, n_far, me, remote, pairs, *refs):
    near, far = refs[0], refs[1 : 1 + n_far]
    rest = refs[1 + n_far :]
    state, stiff1, asm0, asm1, geo, mass, weight, bins, fwd, back, coef, sel, selt = rest[:13]
    part_out, out_near = rest[13], rest[14]
    out_far = rest[15 : 15 + n_far]
    asm, pm = rest[15 + n_far : 17 + n_far], rest[17 + n_far :]
    asm[0][...] = asm0[...]
    asm[1][...] = asm1[...]
    take_rows(remote, me, levels, near, far, asm)
    scale = thrice(STEP * mass[...])
    x = jnp.concatenate([state[:, 512 * c : 512 * c + 512] for c in range(3)], axis=0)
    x = x - scale * (stiff1[...] + lift(asm, selt))
    stiff = stiffness(x, geo, fwd, back, coef)
    store_panels(stiff, None, sel, pm)
    send_rows(remote, me, levels, pm, out_near, out_far)
    asm[0][...] = jnp.zeros_like(asm0)
    asm[1][...] = jnp.zeros_like(asm1)
    pair_rows(pairs, pm, asm)
    part = x - scale * (stiff + lift(asm, selt))
    part_out[...] = part
    total = x + part
    w = weight[...]
    acc = bin_dot([w * total[64 * c : 64 * c + 64] for c in range(3)], bins[...])
    lane = lax.broadcasted_iota(jnp.int32, (K, 128), 1)
    for r, (kind, where) in enumerate(levels):
        if kind == "near":
            j = me[0] ^ where
            got, sent = (lambda a, b: near[j, :, a:b]), (lambda a, b: out_near[j, :, a:b])
        else:
            got = lambda a, b, ref=far[where]: ref[:, a:b]
            sent = lambda a, b, ref=out_far[where]: ref[:, a:b]
        high, bin_low = got(128, 256), got(256, 384)
        share = jnp.where(lane < 64, pltpu.roll(high, 64, 1), high)
        label = jnp.where(lane < 64, bin_low, pltpu.roll(bin_low, 64, 1)).astype(jnp.int32)
        first = sent(0, 128) * share
        second = jnp.where(lane < 64, sent(128, 256) * share, 0.0)
        fields = [jnp.where(lane < 64, first, 0.0), jnp.where(lane < 64, 0.0, first), second]
        acc = acc + bin_dot(fields, label)
    sums = bin_finish(acc)
    for j in range(out_near.shape[0]):
        out_near[j, 0:12, 192:256] = sums[:, 64:128]


def merge_kernel(n_in, near, *refs):
    out = refs[n_in]
    sums = jnp.sum(near[:, :, :], axis=0)
    row = lax.broadcasted_iota(jnp.int32, (K, 128), 0)
    col = lax.broadcasted_iota(jnp.int32, (K, 128), 1)
    r = lax.broadcasted_iota(jnp.int32, (128, 128), 0)
    c = lax.broadcasted_iota(jnp.int32, (128, 128), 1)
    spread = jnp.where((r >= 64) & (r < 96) & ((c & 31) == r - 64), 1.0, 0.0)
    sums = jnp.where((row < 12) & (col >= 64) & (col < 96), sums, 0.0)
    full = jnp.dot(sums, spread, precision=lax.Precision.HIGHEST, preferred_element_type=F32)
    full = jnp.where((row & 3) == (col >> 5), full, 0.0)
    done = jnp.concatenate([jnp.sum(full[4 * i : 4 * i + 4], axis=0, keepdims=True) for i in range(3)], axis=0)
    out[...] = done


def copies_kernel(n_in, sums, *refs):
    out = refs[n_in]
    for j in range(out.shape[0]):
        out[j] = sums[...]


def total_kernel(planes, scale, z, parts, out):
    acc = parts[z[0]]
    for plane in range(1, planes):
        acc = acc + parts[lax.rem(z[0] + (planes - plane), planes)]
    out[...] = acc * scale


def last_kernel(levels, n_far, me, remote, *refs):
    near, far = refs[0], refs[1 : 1 + n_far]
    part, mass, selt, out, *asm = refs[1 + n_far :]
    for block in asm:
        block[...] = jnp.zeros_like(block)
    take_rows(remote, me, levels, near, far, asm)
    moved = part[...] - thrice(STEP * mass[...]) * lift(asm, selt)
    for c in range(3):
        out[:, 512 * c : 512 * c + 512] = moved[64 * c : 64 * c + 64]


SMEM = pl.BlockSpec(memory_space=pltpu.SMEM)
ANY = pl.BlockSpec(memory_space=pl.ANY)
PARAMS = pltpu.CompilerParams(vmem_limit_bytes=56 * 1024 * 1024)


def whole(a):
    return pl.BlockSpec(a.shape, lambda i, n=len(a.shape): (0,) * n)


def call(kernel, name, scalars, arrays, outs, scratch):
    return pl.pallas_call(
        kernel,
        out_shape=outs,
        grid=(1,),
        in_specs=[SMEM] * len(scalars) + [whole(a) for a in arrays],
        out_specs=[whole(a) for a in outs],
        scratch_shapes=scratch,
        compiler_params=PARAMS,
        name=name,
    )(*scalars, *arrays)


def hold_kernel(*refs):
    pass


def hold(arrays):
    n = len(arrays)
    return pl.pallas_call(
        hold_kernel,
        out_shape=[jax.ShapeDtypeStruct(a.shape, a.dtype) for a in arrays],
        in_specs=[ANY] * n,
        out_specs=[ANY] * n,
        input_output_aliases={i: i for i in range(n)},
        cost_estimate=pl.CostEstimate(flops=40_000_000_000, bytes_accessed=0, transcendentals=0),
        name="hold",
    )(*arrays)


def on_device(sizes, state, geo, mass, weight, bins, pairs, remote):
    nz, nx, ny, nc = sizes
    group = ("x", "y", "c")
    n_near = nx * ny * nc
    log = lambda n: n.bit_length() - 1
    n_far = log(nz)
    levels = [("near", ny * nc * 2**b) for b in range(log(nx))]
    levels += [("far", n_far - 1 - b) for b in range(n_far)]
    levels += [("near", 2**b) for b in range(log(ny * nc))]
    fwd, back, coef, sel, selt = (jnp.asarray(a) for a in constants())
    me = lax.axis_index(group).astype(jnp.int32).reshape(1)
    shape = lambda *dims: jax.ShapeDtypeStruct(dims, F32)

    def swap(far, first=0):
        masks = [2 ** (n_far - 1 - first - i) for i in range(len(far))]
        return [lax.ppermute(v, "z", [(s, s ^ m) for s in range(nz)]) for v, m in zip(far, masks)]

    def spread(near):
        return lax.all_to_all(near, group, 0, 0, tiled=True)

    ops = [fwd, back, coef, sel]
    stiff1, asm0, asm1, near, *far = call(
        functools.partial(first_kernel, levels),
        "first",
        [me, remote, pairs.T],
        [state, geo, mass, weight, bins, *ops],
        [shape(192, 512), shape(384, 128), shape(384, 128), shape(n_near, K, 384)]
        + [shape(K, 384)] * n_far,
        [VM((384, 128), F32)] * 3,
    )
    near, far = spread(near), swap(far)
    far = [*hold(far[:1]), *far[1:]]
    part, near, *far = call(
        functools.partial(middle_kernel, levels, n_far),
        "middle",
        [me, remote, pairs.T],
        [near, *far, state, stiff1, asm0, asm1, geo, mass, weight, bins, *ops, selt],
        [shape(192, 512), shape(n_near, K, 256)] + [shape(K, 256)] * n_far,
        [VM((384, 128), F32)] * 4,
    )
    near, late = spread(near), far[2:]
    sums, *late = pl.pallas_call(
        functools.partial(merge_kernel, len(late)),
        out_shape=[shape(3, 128)] + [shape(K, 256)] * len(late),
        grid=(1,),
        in_specs=[pl.BlockSpec((n_near, K, 128), lambda i: (0, 0, 1))] + [ANY] * len(late),
        out_specs=[pl.BlockSpec((3, 128), lambda i: (0, 0))] + [ANY] * len(late),
        input_output_aliases={1 + i: 1 + i for i in range(len(late))},
        compiler_params=PARAMS,
        name="merge",
    )(near, *late)
    hop = [(z * n_near + m, (z + m) % nz * n_near + m) for z in range(nz) for m in range(n_near)]
    sums = lax.ppermute(sums, ("z", *group), hop)
    mids, tail = swap(late[:2], 2), late[2:]
    held = hold(swap(far[:2]))
    gone = [*held, *mids]
    sums, *tail = pl.pallas_call(
        functools.partial(copies_kernel, len(gone) + len(tail)),
        out_shape=[shape(n_near, 3, 128)] + [shape(K, 256)] * len(tail),
        grid=(1,),
        in_specs=[whole(sums)] + [ANY] * (len(gone) + len(tail)),
        out_specs=[pl.BlockSpec((n_near, 3, 128), lambda i: (0, 0, 0))] + [ANY] * len(tail),
        input_output_aliases={1 + len(gone) + i: 1 + i for i in range(len(tail))},
        compiler_params=PARAMS,
        name="copies",
    )(sums, *gone, *tail)
    sums = spread(sums)
    far = [*gone, *swap(tail, 4)]
    (final,) = call(
        functools.partial(last_kernel, levels, n_far),
        "last",
        [me, remote],
        [near, *far, part, mass, selt],
        [shape(E, 1536)],
        [VM((384, 128), F32)] * 2,
    )
    points = nz * n_near * E * 512
    (gradient,) = call(
        functools.partial(total_kernel, nz, 1.0 / math.sqrt(points / NBIN)),
        "total",
        [lax.axis_index("z").astype(jnp.int32).reshape(1)],
        [sums],
        [shape(3, 128)],
        [],
    )
    return final, gradient


def solution(mesh):
    gx, gy = mesh.shape["gx"], mesh.shape["gy"]
    nx = 4 if gx >= 16 else 2
    sizes = (gx // nx, nx, gy // 2, 2)
    names = ("z", "x", "y", "c")
    inner = Mesh(mesh.devices.reshape(sizes), names)
    rows = P(names, None)
    return jax.shard_map(
        functools.partial(on_device, sizes),
        mesh=inner,
        in_specs=(rows,) * 7,
        out_specs=(rows, P()),
        check_vma=False,
    )
```

```python
import functools
import math

import jax
import jax.numpy as jnp
import numpy as np
from jax import lax
from jax.experimental import pallas as pl
from jax.experimental.pallas import tpu as pltpu
from jax.sharding import Mesh
from jax.sharding import PartitionSpec as P

NBIN = 128
STEP = 0.00015
E = 64
K = 24
F32 = jnp.float32
BF16 = jnp.bfloat16
VM = pltpu.VMEM


def cheb():
    m = np.arange(8)
    x = np.cos(np.pi * m / 7.0)
    c = np.where((m == 0) | (m == 7), 2.0, 1.0)
    sign = np.where((m[:, None] + m[None, :]) % 2 == 0, 1.0, -1.0)
    same = m[:, None] == m[None, :]
    gap = np.where(same, 1.0, x[:, None] - x[None, :])
    off = np.where(same, 0.0, c[:, None] / c[None, :] * sign / gap)
    return off - np.diag(off.sum(axis=1))


def split_const(a):
    hi = a.astype(np.float32).astype(jnp.bfloat16)
    lo = (a - hi.astype(np.float64)).astype(np.float32).astype(jnp.bfloat16)
    return hi, lo


def constants():
    d = cheb()
    last = np.kron(np.eye(16), d.T)
    middle = np.kron(np.kron(np.eye(2), d.T), np.eye(8))
    fh, fl = split_const(np.concatenate([last, middle], axis=1))
    forward = np.concatenate([fh, fh, fl], axis=0)
    bh, bl = split_const(np.concatenate([last.T, middle.T], axis=0))
    back = np.concatenate([bh, bl], axis=1)
    rows = []
    for mat in (d, d.T):
        for cross in (0, 1):
            for out in range(4):
                for src in range(4):
                    low = mat[2 * out, 2 * src + cross]
                    high = mat[2 * out + 1, 2 * src + 1 - cross]
                    rows.append(np.repeat([low, high], 64))
    coef = np.stack(rows).astype(np.float32)
    p = np.arange(64)
    u, l = p // 8, p % 8
    targets = np.concatenate(
        [p, 448 + p, u * 64 + l, u * 64 + 56 + l, u * 64 + l * 8, u * 64 + l * 8 + 7]
    )
    sel = np.arange(512)[:, None] == targets[None, :]
    sel = sel.astype(np.float32).astype(jnp.bfloat16)
    return forward, back, coef, sel, np.ascontiguousarray(sel.T)


def split(x):
    hi = x.astype(BF16)
    return hi, (x - hi.astype(F32)).astype(BF16)


def dot(a, b):
    return lax.dot_general(a, b, (((1,), (0,)), ((), ())), preferred_element_type=F32)


def thrice(x):
    return jnp.concatenate([x, x, x], axis=0)


def stiffness(x, geo, fwd, back, coef):
    quads = [x[:, 128 * q : 128 * q + 128] for q in range(4)]
    rows = jnp.concatenate(quads, axis=0)
    hi, lo = split(rows)
    grads = dot(jnp.concatenate([hi, lo], axis=1), fwd[0:256, :]) + dot(hi, fwd[256:384, :])
    scaled = []
    for q in range(4):
        metric = jnp.concatenate(
            [
                geo[:, 1024 + 128 * q : 1152 + 128 * q],
                geo[:, 512 + 128 * q : 640 + 128 * q],
            ],
            axis=1,
        )
        scaled.append(grads[192 * q : 192 * q + 192] * thrice(metric))
    hi, lo = split(jnp.concatenate(scaled, axis=0))
    both = dot(hi, back[...])
    lanes = both[:, :128] + both[:, 128:] + dot(lo, back[:, 0:128])
    out = []
    for part in range(6):
        lo_row = 32 * part
        e0 = lo_row % 64
        xs = [q[lo_row : lo_row + 32] for q in quads]
        rolled = [pltpu.roll(v, 64, 1) for v in xs]
        mids = []
        for o in range(4):
            acc = None
            for s in range(4):
                r = 4 * o + s
                term = coef[r : r + 1, :] * xs[s] + coef[16 + r : 17 + r, :] * rolled[s]
                acc = term if acc is None else acc + term
            mids.append(acc * geo[e0 : e0 + 32, 128 * o : 128 * o + 128])
        rolled = [pltpu.roll(v, 64, 1) for v in mids]
        cols = []
        for o in range(4):
            base = 192 * o + lo_row
            acc = lanes[base : base + 32]
            for s in range(4):
                r = 32 + 4 * o + s
                acc = acc + coef[r : r + 1, :] * mids[s] + coef[16 + r : 17 + r, :] * rolled[s]
            cols.append(acc)
        out.append(jnp.concatenate(cols, axis=1))
    return jnp.concatenate(out, axis=0)


def store_panels(stiff, extra, sel, pm):
    hi, lo = split(stiff)
    stack = [hi, lo]
    if extra is not None:
        weight, bins = extra
        stack += [*split(weight), bins.astype(BF16)]
    got = dot(jnp.concatenate(stack, axis=0), sel[...])
    face = got[0:192] + got[192:384]
    if extra is not None:
        wface = got[384:448] + got[448:512]
        bface = got[512:576]
    zero = jnp.zeros((E, 64), F32)
    for f in range(6):
        cut = slice(64 * f, 64 * f + 64)
        c0, c1, c2 = (face[64 * c : 64 * c + 64, cut] for c in range(3))
        third = zero if extra is None else wface[:, cut]
        pm[0][pl.ds(f, E, stride=6), :] = jnp.concatenate([c0, c1], axis=1)
        pm[1][pl.ds(f, E, stride=6), :] = jnp.concatenate([c2, third], axis=1)
        if extra is not None:
            pm[2][pl.ds(f, E, stride=6), :] = jnp.concatenate([bface[:, cut], zero], axis=1)


def send_rows(remote, me, levels, pm, out_near, out_far):
    for r, (kind, where) in enumerate(levels):
        for k in range(K):
            face = remote[r, k]
            for i, block in enumerate(pm):
                row, lanes = block[pl.ds(face, 1), :], slice(128 * i, 128 * i + 128)
                if kind == "near":
                    out_near[me[0] ^ where, k : k + 1, lanes] = row
                else:
                    out_far[where][k : k + 1, lanes] = row


def take_rows(remote, me, levels, near, far, asm):
    for r, (kind, where) in enumerate(levels):
        for k in range(K):
            face = remote[r, k]
            for i, block in enumerate(asm):
                lanes = slice(128 * i, 128 * i + 128)
                if kind == "near":
                    row = near[me[0] ^ where, k : k + 1, lanes]
                else:
                    row = far[where][k : k + 1, lanes]
                block[pl.ds(face, 1), :] = row


def pair_rows(pairs, pm, asm):
    for i in range(pairs.shape[1]):
        a, b = pairs[0, i], pairs[1, i]
        for source, block in zip(pm, asm):
            block[pl.ds(b, 1), :] = source[pl.ds(a, 1), :]
            block[pl.ds(a, 1), :] = source[pl.ds(b, 1), :]


def lift(asm, selt):
    faces = []
    for f in range(6):
        one = asm[0][pl.ds(f, E, stride=6), :]
        two = asm[1][pl.ds(f, E, stride=6), :]
        faces.append(jnp.concatenate([one[:, 0:64], one[:, 64:128], two[:, 0:64]], axis=0))
    hi, lo = split(jnp.concatenate(faces, axis=1))
    got = dot(jnp.concatenate([hi, lo], axis=0), selt[...])
    return got[0:192] + got[192:384]


def bin_dot(ws, bins):
    groups = bins.shape[0] // 8
    left, right = [], []
    for g in range(groups):
        cut = slice(8 * g, 8 * g + 8)
        b = bins[cut]
        upper, lower = b >> 5, b & 31
        masks = [upper == u for u in range(4)]
        rows = [jnp.where(m, w[cut], 0.0) for w in ws for m in masks]
        left.append(jnp.concatenate(rows, axis=0))
        ones = [jnp.where(lower == v, 1.0, 0.0) for v in range(32)]
        right.append(jnp.concatenate(ones, axis=0).astype(BF16))
    hi, lo = split(jnp.concatenate(left, axis=1))
    return lax.dot_general(
        jnp.concatenate([hi, lo], axis=0),
        jnp.concatenate(right, axis=1),
        (((1,), (1,)), ((), ())),
        preferred_element_type=F32,
    )


def bin_finish(acc):
    row = lax.broadcasted_iota(jnp.int32, (192, 256), 0)
    col = lax.broadcasted_iota(jnp.int32, (192, 256), 1)
    acc = jnp.where((row & 7) == (col & 7), acc, 0.0)
    summed = jnp.sum(acc.reshape(24, 8, 256), axis=1)
    r = lax.broadcasted_iota(jnp.int32, (256, 128), 0)
    c = lax.broadcasted_iota(jnp.int32, (256, 128), 1)
    put = jnp.where((r >> 3) + 64 == c, 1.0, 0.0)
    summed = summed[0:12] + summed[12:24]
    return jnp.dot(summed, put, precision=lax.Precision.HIGHEST, preferred_element_type=F32)


def first_kernel(levels, me, remote, pairs, state, geo, mass, weight, bins, fwd, back, coef, sel, *outs):
    stiff_out, asm0, asm1, out_near, *rest = outs
    out_far, pm = rest[:-3], rest[-3:]
    x = jnp.concatenate([state[:, 512 * c : 512 * c + 512] for c in range(3)], axis=0)
    stiff = stiffness(x, geo, fwd, back, coef)
    stiff_out[...] = stiff
    shares = (-STEP) * weight[...] * mass[...]
    store_panels(stiff, (shares, bins[...].astype(F32)), sel, pm)
    send_rows(remote, me, levels, pm, out_near, out_far)
    asm0[...] = jnp.zeros_like(asm0)
    asm1[...] = jnp.zeros_like(asm1)
    pair_rows(pairs, pm, (asm0, asm1))


def middle_kernel(levels, n_far, me, remote, pairs, *refs):
    near, far = refs[0], refs[1 : 1 + n_far]
    rest = refs[1 + n_far :]
    state, stiff1, asm0, asm1, geo, mass, weight, bins, fwd, back, coef, sel, selt = rest[:13]
    part_out, out_near = rest[13], rest[14]
    out_far = rest[15 : 15 + n_far]
    asm, pm = rest[15 + n_far : 17 + n_far], rest[17 + n_far :]
    asm[0][...] = asm0[...]
    asm[1][...] = asm1[...]
    take_rows(remote, me, levels, near, far, asm)
    scale = thrice(STEP * mass[...])
    x = jnp.concatenate([state[:, 512 * c : 512 * c + 512] for c in range(3)], axis=0)
    x = x - scale * (stiff1[...] + lift(asm, selt))
    stiff = stiffness(x, geo, fwd, back, coef)
    store_panels(stiff, None, sel, pm)
    send_rows(remote, me, levels, pm, out_near, out_far)
    asm[0][...] = jnp.zeros_like(asm0)
    asm[1][...] = jnp.zeros_like(asm1)
    pair_rows(pairs, pm, asm)
    part = x - scale * (stiff + lift(asm, selt))
    part_out[...] = part
    total = x + part
    w = weight[...]
    acc = bin_dot([w * total[64 * c : 64 * c + 64] for c in range(3)], bins[...])
    lane = lax.broadcasted_iota(jnp.int32, (K, 128), 1)
    for r, (kind, where) in enumerate(levels):
        if kind == "near":
            j = me[0] ^ where
            got, sent = (lambda a, b: near[j, :, a:b]), (lambda a, b: out_near[j, :, a:b])
        else:
            got = lambda a, b, ref=far[where]: ref[:, a:b]
            sent = lambda a, b, ref=out_far[where]: ref[:, a:b]
        high, bin_low = got(128, 256), got(256, 384)
        share = jnp.where(lane < 64, pltpu.roll(high, 64, 1), high)
        label = jnp.where(lane < 64, bin_low, pltpu.roll(bin_low, 64, 1)).astype(jnp.int32)
        first = sent(0, 128) * share
        second = jnp.where(lane < 64, sent(128, 256) * share, 0.0)
        fields = [jnp.where(lane < 64, first, 0.0), jnp.where(lane < 64, 0.0, first), second]
        acc = acc + bin_dot(fields, label)
    sums = bin_finish(acc)
    for j in range(out_near.shape[0]):
        out_near[j, 0:12, 192:256] = sums[:, 64:128]


def merge_kernel(copies, n_in, near, *refs):
    out = refs[n_in]
    sums = jnp.sum(near[:, :, :], axis=0)
    row = lax.broadcasted_iota(jnp.int32, (K, 128), 0)
    col = lax.broadcasted_iota(jnp.int32, (K, 128), 1)
    r = lax.broadcasted_iota(jnp.int32, (128, 128), 0)
    c = lax.broadcasted_iota(jnp.int32, (128, 128), 1)
    spread = jnp.where((r >= 64) & (r < 96) & ((c & 31) == r - 64), 1.0, 0.0)
    sums = jnp.where((row < 12) & (col >= 64) & (col < 96), sums, 0.0)
    full = jnp.dot(sums, spread, precision=lax.Precision.HIGHEST, preferred_element_type=F32)
    full = jnp.where((row & 3) == (col >> 5), full, 0.0)
    done = jnp.concatenate([jnp.sum(full[4 * i : 4 * i + 4], axis=0, keepdims=True) for i in range(3)], axis=1)
    for j in range(copies):
        out[j] = done


def last_kernel(levels, n_far, me, remote, *refs):
    near, far = refs[0], refs[1 : 1 + n_far]
    part, mass, selt, out, *asm = refs[1 + n_far :]
    for block in asm:
        block[...] = jnp.zeros_like(block)
    take_rows(remote, me, levels, near, far, asm)
    moved = part[...] - thrice(STEP * mass[...]) * lift(asm, selt)
    for c in range(3):
        out[:, 512 * c : 512 * c + 512] = moved[64 * c : 64 * c + 64]


SMEM = pl.BlockSpec(memory_space=pltpu.SMEM)
ANY = pl.BlockSpec(memory_space=pl.ANY)
PARAMS = pltpu.CompilerParams(vmem_limit_bytes=56 * 1024 * 1024)


def whole(a):
    return pl.BlockSpec(a.shape, lambda i, n=len(a.shape): (0,) * n)


def call(kernel, name, scalars, arrays, outs, scratch):
    return pl.pallas_call(
        kernel,
        out_shape=outs,
        grid=(1,),
        in_specs=[SMEM] * len(scalars) + [whole(a) for a in arrays],
        out_specs=[whole(a) for a in outs],
        scratch_shapes=scratch,
        compiler_params=PARAMS,
        name=name,
    )(*scalars, *arrays)


def hold_kernel(*refs):
    pass


def hold(arrays):
    n = len(arrays)
    return pl.pallas_call(
        hold_kernel,
        out_shape=[jax.ShapeDtypeStruct(a.shape, a.dtype) for a in arrays],
        in_specs=[ANY] * n,
        out_specs=[ANY] * n,
        input_output_aliases={i: i for i in range(n)},
        cost_estimate=pl.CostEstimate(flops=40_000_000_000, bytes_accessed=0, transcendentals=0),
        name="hold",
    )(*arrays)


def on_device(sizes, state, geo, mass, weight, bins, pairs, remote):
    nz, nx, ny, nc = sizes
    group = ("x", "y", "c")
    n_near = nx * ny * nc
    log = lambda n: n.bit_length() - 1
    n_far = log(nz)
    levels = [("near", ny * nc * 2**b) for b in range(log(nx))]
    levels += [("far", n_far - 1 - b) for b in range(n_far)]
    levels += [("near", 2**b) for b in range(log(ny * nc))]
    fwd, back, coef, sel, selt = (jnp.asarray(a) for a in constants())
    me = lax.axis_index(group).astype(jnp.int32).reshape(1)
    shape = lambda *dims: jax.ShapeDtypeStruct(dims, F32)

    def swap(far, first=0):
        masks = [2 ** (n_far - 1 - first - i) for i in range(len(far))]
        return [lax.ppermute(v, "z", [(s, s ^ m) for s in range(nz)]) for v, m in zip(far, masks)]

    def spread(near):
        return lax.all_to_all(near, group, 0, 0, tiled=True)

    ops = [fwd, back, coef, sel]
    stiff1, asm0, asm1, near, *far = call(
        functools.partial(first_kernel, levels),
        "first",
        [me, remote, pairs.T],
        [state, geo, mass, weight, bins, *ops],
        [shape(192, 512), shape(384, 128), shape(384, 128), shape(n_near, K, 384)]
        + [shape(K, 384)] * n_far,
        [VM((384, 128), F32)] * 3,
    )
    near, far = spread(near), swap(far)
    far = [*hold(far[:1]), *far[1:]]
    part, near, *far = call(
        functools.partial(middle_kernel, levels, n_far),
        "middle",
        [me, remote, pairs.T],
        [near, *far, state, stiff1, asm0, asm1, geo, mass, weight, bins, *ops, selt],
        [shape(192, 512), shape(n_near, K, 256)] + [shape(K, 256)] * n_far,
        [VM((384, 128), F32)] * 4,
    )
    near, late = spread(near), far[2:]
    sums, *late = pl.pallas_call(
        functools.partial(merge_kernel, nz, len(late)),
        out_shape=[shape(nz, 1, 384)] + [shape(K, 256)] * len(late),
        grid=(1,),
        in_specs=[pl.BlockSpec((n_near, K, 128), lambda i: (0, 0, 1))] + [ANY] * len(late),
        out_specs=[pl.BlockSpec((nz, 1, 384), lambda i: (0, 0, 0))] + [ANY] * len(late),
        input_output_aliases={1 + i: 1 + i for i in range(len(late))},
        compiler_params=PARAMS,
        name="merge",
    )(near, *late)
    sums = lax.all_to_all(sums, "z", 0, 0, tiled=True)
    far = [*hold(swap(far[:2])), *swap(late, 2)]
    (final,) = call(
        functools.partial(last_kernel, levels, n_far),
        "last",
        [me, remote],
        [near, *far, part, mass, selt],
        [shape(E, 1536)],
        [VM((384, 128), F32)] * 2,
    )
    points = nz * n_near * E * 512
    return final, jnp.sum(sums, axis=0).reshape(3, 128) * (1.0 / math.sqrt(points / NBIN))


def solution(mesh):
    gx, gy = mesh.shape["gx"], mesh.shape["gy"]
    nx = 4 if gx >= 16 else 2
    sizes = (gx // nx, nx, gy // 2, 2)
    names = ("z", "x", "y", "c")
    inner = Mesh(mesh.devices.reshape(sizes), names)
    rows = P(names, None)
    return jax.shard_map(
        functools.partial(on_device, sizes),
        mesh=inner,
        in_specs=(rows,) * 7,
        out_specs=(rows, P()),
        check_vma=False,
    )
```
